512 devices in a mesh: energy: 64 (over y_hi, z, core), slab: 8 (over y_lo, x).
Axes of the slice: x: 4, y: 8 (y_hi: 4, y_lo: 2; y = y_hi * 2 + y_lo), z: 8, core: 2. Of those that a mesh axis runs over, the one named last changes fastest.
Arguments:
- green: bfloat16 [64, 32, 512, 512], P('energy', 'slab'), may hold values from -6 to 6
- coupling: bfloat16 [32, 3, 512, 512], P('slab'), may hold values from -0.25 to 0.25
- bonds: int32 [32, 3], P('slab'), may hold values from 0 to 31, as said below
- counts: int32 [64], P('energy'), may hold values from 1 to 32
- bose: float32 [1], replicated, may hold values from 0.3 to 2
Outputs:
- sigma: bfloat16 [64, 32, 512, 512], P('energy', 'slab')
The draws below stay inside these ranges and needn't reach their ends.
Inputs may be any that keep to these rules, and one draw needn't show every extreme that they name: `bonds`: the first bond of a block reaches the block itself; the other two reach the block just before or just after it, different blocks where both exist, else both the single neighbour.
All inputs are finite; a program needn't handle non-finite values.
Results may differ from the reference program's by a relative error of at most 0.0057.
Values may be sent and summed in bfloat16 or wider, within the bound.
A program may use at most 64 MiB of HBM per device.

```python
import jax
import jax.numpy as jnp
from jax import lax

ORB = 512
BONDS = 3
OFF = 8
ENERGIES = 64
BLOCKS = 32


def draw_bonds(key, part):
    key = jax.random.fold_in(key, 11)
    sign = jax.random.randint(key, (BLOCKS,), 0, 2) * 2 - 1
    base = jnp.arange(BLOCKS, dtype=jnp.int32)
    first = base + sign
    second = base - sign
    first = jnp.where(first < 0, 1, jnp.where(first > BLOCKS - 1, BLOCKS - 2, first))
    second = jnp.where(second < 0, 1, jnp.where(second > BLOCKS - 1, BLOCKS - 2, second))
    return jnp.stack([base, first, second], axis=1).astype(jnp.int32)


def draw_counts(key, part):
    key = jax.random.fold_in(key, 12)
    values = jax.random.randint(key, (ENERGIES,), 1, BLOCKS + 1)
    values = values.at[0].set(BLOCKS)
    values = values.at[ENERGIES - 1].set(1)
    return values.astype(jnp.int32)


def block_levels(key, shape, cuts, least, high):
    def one(position, blocks):
        steps = jax.random.uniform(jax.random.fold_in(jax.random.fold_in(key, 6), position), (blocks,), jnp.float32, least / len(cuts), high / len(cuts))
        return jnp.repeat(jnp.exp(steps), shape[position] // blocks).reshape((-1,) + (1,) * (len(shape) - position - 1))

    level = one(*cuts[0])
    for cut in cuts[1:]:
        level = level * one(*cut)
    return level


def noise(rng, dims, scale, bound, pieces=(), kind=jnp.bfloat16):
    array = scale * jax.random.normal(rng, dims, jnp.float32)
    if pieces:
        array = array * block_levels(rng, dims, pieces, -0.22, 0.18)
    return jnp.clip(array, -bound, bound).astype(kind)


def setup_inputs(seed: int = 0) -> dict:
    splits = jax.random.split(jax.random.key(seed), 6)
    return {
        "green": noise(splits[0], (ENERGIES, BLOCKS, ORB, ORB), 1.0, 6.0, ((0, 64), (1, 8))),
        "coupling": noise(splits[1], (BLOCKS, BONDS, ORB, ORB), ORB ** -0.5, 0.25, ((0, 8),)),
        "bonds": draw_bonds(jax.random.fold_in(splits[5], 71), 0),
        "counts": draw_counts(jax.random.fold_in(splits[5], 71), 0),
        "bose": jnp.clip(jax.random.uniform(splits[4], (1,), jnp.float32, 0.3, 2.0), 0.3, 2.0),
    }


def energy_part(green_one, coupling, bonds):
    near = jnp.take(green_one, bonds.reshape(-1), axis=0).reshape(BLOCKS, BONDS, ORB, ORB)
    left = jnp.einsum('bkij,bkjl->bkil', coupling.astype(jnp.float32), near.astype(jnp.float32)).astype(jnp.bfloat16)
    part = jnp.einsum('bkil,bkml->bim', left.astype(jnp.float32), coupling.astype(jnp.float32))
    return part.astype(jnp.bfloat16)


def reference(green, coupling, bonds, counts, bose):
    part = lax.map(lambda green_one: energy_part(green_one, coupling, bonds), green)
    zeros = jnp.zeros((OFF, BLOCKS, ORB, ORB), jnp.bfloat16)
    above = jnp.concatenate([part[OFF:], zeros], axis=0)
    below = jnp.concatenate([zeros, part[:ENERGIES - OFF]], axis=0)
    occupation = bose[0]
    active = (jnp.arange(BLOCKS, dtype=jnp.int32)[None, :] < counts[:, None]).astype(jnp.float32)
    total = (occupation + 1.0) * above.astype(jnp.float32) + occupation * below.astype(jnp.float32)
    return (total * active[:, :, None, None]).astype(jnp.bfloat16)
```

```python
import functools

import jax
import jax.numpy as jnp
from jax import lax
from jax.experimental import pallas as pl
from jax.experimental.pallas import tpu as pltpu
from jax.sharding import PartitionSpec as P

OFF = 8
MESH = pl.DeviceIdType.MESH
MIB = 2**20


def kernel(
    energies, slabs, rows,
    green, coupling, bonds, counts, bose, sigma,
    g, before, after, c0, c1, c2, c3,
    part_z, part_y, got_z, got_q, got_y, sig_z, sig_own, cnt_own, cnt_got,
    load_sem, halo_send, halo_recv, cnt_sem,
    z_send, z_recv, q_send, q_recv, y_send, y_recv, o_send, o_recv, w_sem,
):
    e = lax.axis_index("energy")
    s = lax.axis_index("slab")
    orb = g.shape[-1]
    tiles = orb // rows
    n_tiles = 2 * tiles
    upper = (e // OFF) % 2
    partner = e + OFF - 2 * OFF * upper
    up = (e + 2 * OFF) % energies
    down = (e + energies - 2 * OFF) % energies
    y_to = jnp.where(upper == 0, down, up)
    q_to = jnp.where(upper == 0, up, down)
    left = (s + slabs - 1) % slabs
    right = (s + 1) % slabs

    barrier = pltpu.get_barrier_semaphore()
    for device in ((partner, s), (up, s), (down, s), (e, left), (e, right)):
        pl.semaphore_signal(barrier, inc=1, device_id=device, device_id_type=MESH)

    blocks = (c0, c1, c2, c3)
    loads = [pltpu.make_async_copy(green.at[0], g, load_sem.at[4])]
    loads += [pltpu.make_async_copy(coupling.at[b], blocks[b], load_sem.at[b]) for b in range(4)]
    for i in (0, 2, 3, 1, 4):
        loads[i].start()

    cnt_own[...] = jnp.full(cnt_own.shape, counts[0], jnp.int32)

    def remote(src, dst, send, recv, device):
        return pltpu.make_async_remote_copy(
            src_ref=src, dst_ref=dst, send_sem=send, recv_sem=recv,
            device_id=device, device_id_type=MESH,
        )

    to_right = remote(green.at[0, 3], before, halo_send.at[0], halo_recv.at[0], (e, right))
    to_left = remote(green.at[0, 0], after, halo_send.at[1], halo_recv.at[1], (e, left))
    edge_before = pltpu.make_async_copy(green.at[0, 1], before, halo_recv.at[0])
    edge_after = pltpu.make_async_copy(green.at[0, 2], after, halo_recv.at[1])
    count = remote(cnt_own, cnt_got, cnt_sem.at[0], cnt_sem.at[1], (partner, s))

    def place(i):
        return i // tiles, pl.ds(pl.multiple_of((i % tiles) * rows, rows), rows)

    def z_copy(i):
        j, r = place(i)
        return remote(part_z.at[j, r], got_z.at[j, r], z_send.at[i], z_recv.at[i], (partner, s))

    def q_copy(i):
        j, r = place(i)
        return remote(got_z.at[j, r], got_q.at[j, r], q_send.at[i], q_recv.at[i], (q_to, s))

    def y_copy(i):
        j, r = place(i)
        return remote(part_y.at[j, r], got_y.at[j, r], y_send.at[i], y_recv.at[i], (y_to, s))

    def o_copy(i):
        j, r = place(i)
        return remote(sig_z.at[j, r], sigma.at[0, 3 * j, r], o_send.at[i], o_recv.at[i], (partner, s))

    def w_copy(i):
        j, r = place(i)
        return pltpu.make_async_copy(sig_own.at[j, r], sigma.at[0, 1 + j, r], w_sem.at[i])

    def products(b, r, lower, higher):
        c = blocks[b]
        k = 1 + (bonds[b, 1] > bonds[b, 0]).astype(jnp.int32)
        total = None
        for k, near in ((0, g.at[b]), (k, lower), (3 - k, higher)):
            half = jnp.dot(c[k, r, :], near[...], preferred_element_type=jnp.float32)
            term = lax.dot_general(
                half.astype(jnp.bfloat16), c[k], (((1,), (1,)), ((), ())),
                preferred_element_type=jnp.float32,
            )
            total = term if total is None else total + term
        return total.astype(jnp.bfloat16)

    loads[0].wait()
    for j in (0, 1):
        loads[2 + j].wait()

        def inner(t, _, j=j):
            i = j * tiles + t
            _, r = place(i)
            part_z[j, r, :] = products(1 + j, r, g.at[j], g.at[2 + j])

            if j == 0:
                @pl.when(t == 0)
                def _():
                    pl.semaphore_wait(barrier, 5)

                    @pl.when(s < slabs - 1)
                    def _():
                        to_right.start()

                    @pl.when(s > 0)
                    def _():
                        to_left.start()

                    count.start()

            z_copy(i).start()
            return 0

        lax.fori_loop(0, tiles, inner, 0)

    @pl.when(s == 0)
    def _():
        edge_before.start()

    @pl.when(s == slabs - 1)
    def _():
        edge_after.start()

    for j, (lower, higher, edge, b) in enumerate(
        ((before, g.at[1], to_right, 0), (g.at[2], after, to_left, 3))
    ):
        edge.wait_recv()
        loads[1 if b == 0 else 4].wait()

        def outer(t, _, j=j, lower=lower, higher=higher, b=b):
            i = j * tiles + t
            _, r = place(i)
            part_y[j, r, :] = products(b, r, lower, higher)
            y_copy(i).start()
            return 0

        lax.fori_loop(0, tiles, outer, 0)

    n = bose[0]
    has_up = e + 2 * OFF < energies
    has_down = e >= 2 * OFF
    y_own = jnp.where(upper == 0, n, n + 1.0)
    y_far = jnp.where(upper == 0, jnp.where(has_up, n + 1.0, 0.0), jnp.where(has_down, n, 0.0))
    q_own = jnp.where(upper == 0, n + 1.0, n)
    q_far = jnp.where(upper == 0, jnp.where(has_down, n, 0.0), jnp.where(has_up, n + 1.0, 0.0))
    count.wait_recv()

    def combine(own, far, own_factor, far_factor, cnt, block):
        active = cnt[0:1, :] > block
        total = own_factor * own.astype(jnp.float32) + far_factor * far.astype(jnp.float32)
        return jnp.where(active, total, 0.0).astype(jnp.bfloat16)

    def middle(i, _):
        j, r = place(i)
        z_copy(i).wait_recv()
        q_copy(i).start()
        y_copy(i).wait_recv()
        sig_z[j, r, :] = combine(part_y[j, r, :], got_y[j, r, :], y_own, y_far, cnt_got, s * 4 + 3 * j)
        o_copy(i).start()
        return 0

    lax.fori_loop(0, n_tiles, middle, 0)

    def last(i, _):
        j, r = place(i)
        q_copy(i).wait_recv()
        sig_own[j, r, :] = combine(got_z[j, r, :], got_q[j, r, :], q_own, q_far, cnt_own, s * 4 + 1 + j)
        w_copy(i).start()
        return 0

    lax.fori_loop(0, n_tiles, last, 0)

    @pl.when(s < slabs - 1)
    def _():
        to_right.wait_send()

    @pl.when(s > 0)
    def _():
        to_left.wait_send()

    count.wait_send()

    def finish(i, _):
        z_copy(i).wait_send()
        q_copy(i).wait_send()
        y_copy(i).wait_send()
        o_copy(i).wait_send()
        w_copy(i).wait()
        o_copy(i).wait_recv()
        return 0

    lax.fori_loop(0, n_tiles, finish, 0)


def solution(mesh):
    energies, slabs = mesh.shape["energy"], mesh.shape["slab"]

    def on_device(green, coupling, bonds, counts, bose):
        orb = green.shape[-1]
        rows = 128
        n_tiles = 2 * (orb // rows)
        block = (orb, orb)
        dma = pltpu.SemaphoreType.DMA
        pair = pltpu.VMEM((2,) + block, jnp.bfloat16)
        hbm = pl.BlockSpec(memory_space=pl.ANY)
        smem = pl.BlockSpec(memory_space=pltpu.SMEM)
        return pl.pallas_call(
            functools.partial(kernel, energies, slabs, rows),
            out_shape=jax.ShapeDtypeStruct(green.shape, jnp.bfloat16),
            in_specs=[hbm, hbm, smem, smem, smem],
            out_specs=hbm,
            scratch_shapes=[
                pltpu.VMEM((4,) + block, jnp.bfloat16),
                pltpu.VMEM(block, jnp.bfloat16),
                pltpu.VMEM(block, jnp.bfloat16),
            ]
            + [pltpu.VMEM((3,) + block, jnp.bfloat16)] * 4
            + [pair] * 7
            + [pltpu.VMEM((8, orb), jnp.int32)] * 2
            + [dma((5,)), dma((2,)), dma((2,)), dma((2,))]
            + [dma((n_tiles,))] * 9,
            compiler_params=pltpu.CompilerParams(
                collective_id=0, has_side_effects=True, vmem_limit_bytes=60 * MIB
            ),
            cost_estimate=pl.CostEstimate(
                flops=48 * orb**3, bytes_accessed=20 * MIB, transcendentals=0
            ),
            name="self_energy",
        )(green, coupling, bonds, counts, bose)

    return jax.shard_map(
        on_device,
        mesh=mesh,
        in_specs=(
            P("energy", "slab", None, None),
            P("slab", None, None, None),
            P("slab", None),
            P("energy"),
            P(),
        ),
        out_specs=P("energy", "slab", None, None),
        check_vma=False,
    )
```

```python
import functools

import jax
import jax.numpy as jnp
from jax import lax
from jax.experimental import pallas as pl
from jax.experimental.pallas import tpu as pltpu
from jax.sharding import PartitionSpec as P

OFF = 8
ROWS = 128
MESH = pl.DeviceIdType.MESH
MIB = 2**20
ORDER = (1, 2, 0, 3)


def kernel(
    energies, slabs,
    green, coupling, bonds_hbm, counts_hbm, bose_hbm, sigma,
    g, before, after, c0, c1, c2, c3,
    part, got_z, got_q, got_y, sig, cnt_own, cnt_got, bonds, counts, bose,
    load_sem, small_sem, halo_send, halo_recv, cnt_sem, y_ok, q_ok,
    z_send, z_recv, q_send, q_recv, y_send, y_recv, o_send, o_recv,
):
    e = lax.axis_index("energy")
    s = lax.axis_index("slab")
    orb = g.shape[-1]
    per = orb // ROWS
    upper = (e // OFF) % 2
    late = (e // 4) % 2 == 1
    early = jnp.logical_not(late)
    partner = e + OFF - 2 * OFF * upper
    up = (e + 2 * OFF) % energies
    down = (e + energies - 2 * OFF) % energies
    y_to = jnp.where(upper == 0, down, up)
    q_to = jnp.where(upper == 0, up, down)
    left = (s + slabs - 1) % slabs
    right = (s + 1) % slabs

    barrier = pltpu.get_barrier_semaphore()
    peers = [(partner, s), (up, s), (down, s), (e, left), (e, right)]
    for device in peers:
        pl.semaphore_signal(barrier, inc=1, device_id=device, device_id_type=MESH)

    blocks = (c0, c1, c2, c3)
    small = [
        pltpu.make_async_copy(src, dst, small_sem.at[i])
        for i, (src, dst) in enumerate(((bonds_hbm, bonds), (counts_hbm, counts), (bose_hbm, bose)))
    ]
    for copy in small:
        copy.start()
    load_g = [pltpu.make_async_copy(green.at[0, b], g.at[b], load_sem.at[b]) for b in range(4)]
    load_c = [pltpu.make_async_copy(coupling.at[b], blocks[b], load_sem.at[4 + b]) for b in range(4)]
    for copy in (load_g[1], load_c[1], load_g[0], load_g[2], load_c[2], load_g[3], load_c[0], load_c[3]):
        copy.start()
    for copy in small:
        copy.wait()
    cnt_own[...] = jnp.full(cnt_own.shape, counts[0], jnp.int32)

    def remote(src, dst, send, recv, device):
        return pltpu.make_async_remote_copy(
            src_ref=src, dst_ref=dst, send_sem=send, recv_sem=recv,
            device_id=device, device_id_type=MESH,
        )

    to_right = remote(green.at[0, 3], before, halo_send.at[0], halo_recv.at[0], (e, right))
    to_left = remote(green.at[0, 0], after, halo_send.at[1], halo_recv.at[1], (e, left))
    edge_before = pltpu.make_async_copy(green.at[0, 1], before, halo_recv.at[0])
    edge_after = pltpu.make_async_copy(green.at[0, 2], after, halo_recv.at[1])
    count = remote(cnt_own, cnt_got, cnt_sem.at[0], cnt_sem.at[1], (partner, s))

    def rows_of(t):
        return t // per, pl.ds(pl.multiple_of((t % per) * ROWS, ROWS), ROWS)

    def block_of(j):
        return jnp.where(j < 2, j + 1, jnp.where(j == 2, 0, 3))

    def z_copy(t):
        j, r = rows_of(t)
        return remote(part.at[j, r], got_z.at[j, r], z_send.at[t], z_recv.at[t], (partner, s))

    def q_copy(t):
        j, r = rows_of(t)
        return remote(got_z.at[j, r], got_q.at[j, r], q_send.at[t], q_recv.at[t], (q_to, s))

    def y_copy(t):
        j, r = rows_of(t)
        return remote(part.at[j, r], got_y.at[j, r], y_send.at[t], y_recv.at[t], (y_to, s))

    def o_copy(t):
        j, r = rows_of(t)
        return remote(sig.at[j, r], sigma.at[0, block_of(j), r], o_send.at[t], o_recv.at[t], (partner, s))

    def z_first(t):
        return jnp.where(early, t // per != 2, t // per == 3)

    def when(flag, action):
        @pl.when(flag)
        def _():
            action()

    def loop(first, last, body):
        def step(t, _):
            body(t)
            return 0

        lax.fori_loop(first, last, step, 0)

    def products(b, r, lower, higher):
        c = blocks[b]
        k = 1 + (bonds[b, 1] > bonds[b, 0]).astype(jnp.int32)
        total = None
        for k, near in ((0, g.at[b]), (k, lower), (3 - k, higher)):
            half = jnp.dot(c[k, r, :], near[...], preferred_element_type=jnp.float32)
            term = lax.dot_general(
                half.astype(jnp.bfloat16), c[k], (((1,), (1,)), ((), ())),
                preferred_element_type=jnp.float32,
            )
            total = term if total is None else total + term
        return total.astype(jnp.bfloat16)

    def first_sends():
        pl.semaphore_wait(barrier, len(peers))
        when(s < slabs - 1, to_right.start)
        when(s > 0, to_left.start)
        count.start()

    def work(j, lower, higher):
        def tile(t):
            _, r = rows_of(t)
            part[j, r, :] = products(ORDER[j], r, lower, higher)
            if j == 0:
                when(t == 0, first_sends)
            if j == 2:
                y_copy(t).start()
            else:
                when(early, z_copy(t).start)

        loop(j * per, (j + 1) * per, tile)

    def forward(t):
        z_copy(t).wait_recv()
        q_copy(t).start()

    for b in (1, 0, 2):
        load_g[b].wait()
    load_c[1].wait()
    work(0, g.at[0], g.at[2])
    load_g[3].wait()
    load_c[2].wait()
    work(1, g.at[1], g.at[3])
    when(s == 0, edge_before.start)
    when(s == slabs - 1, edge_after.start)
    to_right.wait_recv()
    to_left.wait_recv()
    pl.semaphore_signal(y_ok, inc=1, device_id=(q_to, s), device_id_type=MESH)
    pl.semaphore_signal(q_ok, inc=1, device_id=(y_to, s), device_id_type=MESH)
    pl.semaphore_wait(y_ok, 1)
    pl.semaphore_wait(q_ok, 1)
    when(late, lambda: loop(0, 2 * per, lambda t: y_copy(t).start()))
    when(early, lambda: loop(0, 3, forward))
    load_c[0].wait()
    work(2, before, g.at[1])
    load_c[3].wait()
    work(3, g.at[2], after)

    n = bose[0]
    has_up = e + 2 * OFF < energies
    has_down = e >= 2 * OFF
    y_own = jnp.where(upper == 0, n, n + 1.0)
    y_far = jnp.where(upper == 0, jnp.where(has_up, n + 1.0, 0.0), jnp.where(has_down, n, 0.0))
    q_own = jnp.where(upper == 0, n + 1.0, n)
    q_far = jnp.where(upper == 0, jnp.where(has_down, n, 0.0), jnp.where(has_up, n + 1.0, 0.0))

    def combine(own, far, own_factor, far_factor, cnt, block):
        active = cnt[0:1, :] > block
        total = own_factor * own.astype(jnp.float32) + far_factor * far.astype(jnp.float32)
        return jnp.where(active, total, 0.0).astype(jnp.bfloat16)

    def across(t):
        j, r = rows_of(t)
        y_copy(t).wait_recv()
        sig[j, r, :] = combine(part[j, r, :], got_y[j, r, :], y_own, y_far, cnt_got, s * 4 + block_of(j))
        o_copy(t).start()

    count.wait_recv()
    period = 2 * per

    def early_part():
        loop(3, 8, forward)
        loop(8, 10, across)
        loop(12, 14, forward)
        loop(10, 12, across)
        loop(14, 16, forward)

    def late_part():
        loop(12, 16, lambda t: z_copy(t).start())
        loop(0, 6, across)
        loop(12, 14, forward)
        loop(6, 8, across)
        loop(14, 16, forward)
        loop(8, 12, across)

    when(early, early_part)
    when(late, late_part)

    def own(t):
        def action():
            j, r = rows_of(t)
            q_copy(t).wait_recv()
            sigma[0, block_of(j), r, :] = combine(
                got_z[j, r, :], got_q[j, r, :], q_own, q_far, cnt_own, s * 4 + block_of(j)
            )

        when(z_first(t), action)

    loop(0, 2 * period, own)

    when(s < slabs - 1, to_right.wait_send)
    when(s > 0, to_left.wait_send)
    count.wait_send()

    def finish(t):
        def z_way():
            z_copy(t).wait_send()
            q_copy(t).wait_send()

        def y_way():
            y_copy(t).wait_send()
            o_copy(t).wait_send()
            o_copy(t).wait_recv()

        when(z_first(t), z_way)
        when(jnp.logical_not(z_first(t)), y_way)

    loop(0, 2 * period, finish)


def solution(mesh):
    energies, slabs = mesh.shape["energy"], mesh.shape["slab"]

    def on_device(green, coupling, bonds, counts, bose):
        orb = green.shape[-1]
        tiles = 4 * (orb // ROWS)
        block = (orb, orb)
        dma = pltpu.SemaphoreType.DMA
        whole = pltpu.VMEM((4,) + block, jnp.bfloat16)
        hbm = pl.BlockSpec(memory_space=pltpu.HBM)
        return pl.pallas_call(
            functools.partial(kernel, energies, slabs),
            out_shape=pltpu.VMEM(green.shape, jnp.bfloat16),
            in_specs=[hbm] * 5,
            out_specs=pl.BlockSpec(memory_space=pltpu.VMEM),
            scratch_shapes=[
                whole,
                pltpu.VMEM(block, jnp.bfloat16),
                pltpu.VMEM(block, jnp.bfloat16),
            ]
            + [pltpu.VMEM((3,) + block, jnp.bfloat16)] * 4
            + [whole] * 5
            + [pltpu.VMEM((8, orb), jnp.int32)] * 2
            + [pltpu.SMEM(bonds.shape, jnp.int32), pltpu.SMEM((1,), jnp.int32), pltpu.SMEM((1,), jnp.float32)]
            + [dma((8,)), dma((3,)), dma((2,)), dma((2,)), dma((2,))] + [pltpu.SemaphoreType.REGULAR] * 2
            + [dma((tiles,))] * 8,
            compiler_params=pltpu.CompilerParams(
                collective_id=0, has_side_effects=True, vmem_limit_bytes=60 * MIB
            ),
            cost_estimate=pl.CostEstimate(
                flops=48 * orb**3, bytes_accessed=20 * MIB, transcendentals=0
            ),
            name="self_energy",
        )(green, coupling, bonds, counts, bose)

    return jax.shard_map(
        on_device,
        mesh=mesh,
        in_specs=(
            P("energy", "slab", None, None),
            P("slab", None, None, None),
            P("slab", None),
            P("energy"),
            P(),
        ),
        out_specs=P("energy", "slab", None, None),
        check_vma=False,
    )
```

```python
import functools

import jax
import jax.numpy as jnp
from jax import lax
from jax.experimental import pallas as pl
from jax.experimental.pallas import tpu as pltpu
from jax.sharding import PartitionSpec as P

OFF = 8
ROWS = 128
MESH = pl.DeviceIdType.MESH
MIB = 2**20
ORDER = (1, 2, 0, 3)


def kernel(
    energies, slabs,
    green, coupling, bonds_hbm, counts_hbm, bose_hbm, sigma,
    g, before, after, c0, c1, c2, c3,
    part, got_z, got_q, got_y, sig, cnt_own, cnt_got, bonds, counts, bose,
    load_sem, small_sem, halo_send, halo_recv, cnt_sem, y_ok, q_ok,
    z_send, z_recv, q_send, q_recv, y_send, y_recv, o_send, o_recv,
):
    e = lax.axis_index("energy")
    s = lax.axis_index("slab")
    orb = g.shape[-1]
    per = orb // ROWS
    upper = (e // OFF) % 2
    late = (e // 4) % 2 == 1
    early = jnp.logical_not(late)
    partner = e + OFF - 2 * OFF * upper
    up = (e + 2 * OFF) % energies
    down = (e + energies - 2 * OFF) % energies
    y_to = jnp.where(upper == 0, down, up)
    q_to = jnp.where(upper == 0, up, down)
    left = (s + slabs - 1) % slabs
    right = (s + 1) % slabs

    barrier = pltpu.get_barrier_semaphore()
    peers = [(partner, s), (up, s), (down, s), (e, left), (e, right)]
    for device in peers:
        pl.semaphore_signal(barrier, inc=1, device_id=device, device_id_type=MESH)

    blocks = (c0, c1, c2, c3)
    small = [
        pltpu.make_async_copy(src, dst, small_sem.at[i])
        for i, (src, dst) in enumerate(((bonds_hbm, bonds), (counts_hbm, counts), (bose_hbm, bose)))
    ]
    for copy in small:
        copy.start()
    load_g = [pltpu.make_async_copy(green.at[0, b], g.at[b], load_sem.at[b]) for b in range(4)]
    load_c = [pltpu.make_async_copy(coupling.at[b], blocks[b], load_sem.at[4 + b]) for b in range(4)]
    for copy in (load_g[1], load_c[1], load_g[0], load_g[2]):
        copy.start()
    for copy in small:
        copy.wait()
    cnt_own[...] = jnp.full(cnt_own.shape, counts[0], jnp.int32)

    def remote(src, dst, send, recv, device):
        return pltpu.make_async_remote_copy(
            src_ref=src, dst_ref=dst, send_sem=send, recv_sem=recv,
            device_id=device, device_id_type=MESH,
        )

    to_right = remote(green.at[0, 3], before, halo_send.at[0], halo_recv.at[0], (e, right))
    to_left = remote(green.at[0, 0], after, halo_send.at[1], halo_recv.at[1], (e, left))
    edge_before = pltpu.make_async_copy(green.at[0, 1], before, halo_recv.at[0])
    edge_after = pltpu.make_async_copy(green.at[0, 2], after, halo_recv.at[1])
    count = remote(cnt_own, cnt_got, cnt_sem.at[0], cnt_sem.at[1], (partner, s))

    def rows_of(t):
        return t // per, pl.ds(pl.multiple_of((t % per) * ROWS, ROWS), ROWS)

    def block_of(j):
        return jnp.where(j < 2, j + 1, jnp.where(j == 2, 0, 3))

    def z_copy(t):
        j, r = rows_of(t)
        return remote(part.at[j, r], got_z.at[j, r], z_send.at[t], z_recv.at[t], (partner, s))

    def q_copy(t):
        j, r = rows_of(t)
        return remote(got_z.at[j, r], got_q.at[j, r], q_send.at[t], q_recv.at[t], (q_to, s))

    def y_copy(t):
        j, r = rows_of(t)
        return remote(part.at[j, r], got_y.at[j, r], y_send.at[t], y_recv.at[t], (y_to, s))

    def o_copy(t):
        j, r = rows_of(t)
        return remote(sig.at[j, r], sigma.at[0, block_of(j), r], o_send.at[t], o_recv.at[t], (partner, s))

    def z_first(t):
        return jnp.where(early, t // per != 2, t // per == 0)

    def when(flag, action):
        @pl.when(flag)
        def _():
            action()

    def loop(first, last, body):
        def step(t, _):
            body(t)
            return 0

        lax.fori_loop(first, last, step, 0)

    def products(b, r, lower, higher):
        c = blocks[b]
        k = 1 + (bonds[b, 1] > bonds[b, 0]).astype(jnp.int32)
        total = None
        for k, near in ((0, g.at[b]), (k, lower), (3 - k, higher)):
            half = jnp.dot(c[k, r, :], near[...], preferred_element_type=jnp.float32)
            term = lax.dot_general(
                half.astype(jnp.bfloat16), c[k], (((1,), (1,)), ((), ())),
                preferred_element_type=jnp.float32,
            )
            total = term if total is None else total + term
        return total.astype(jnp.bfloat16)

    def first_sends():
        pl.semaphore_wait(barrier, len(peers))
        when(s < slabs - 1, to_right.start)
        when(s > 0, to_left.start)
        count.start()

    def work(j, lower, higher):
        def tile(t):
            _, r = rows_of(t)
            part[j, r, :] = products(ORDER[j], r, lower, higher)
            if j == 0:
                when(t == 0, first_sends)
            if j == 0:
                z_copy(t).start()
            elif j == 2:
                y_copy(t).start()
            else:
                when(early, z_copy(t).start)
                if j == 3:
                    when(late, y_copy(t).start)

        loop(j * per, (j + 1) * per, tile)

    def forward(t):
        z_copy(t).wait_recv()
        q_copy(t).start()

    for b in (1, 0, 2):
        load_g[b].wait()
    load_c[1].wait()
    for copy in (load_c[2], load_g[3], load_c[0], load_c[3]):
        copy.start()
    work(0, g.at[0], g.at[2])
    load_g[3].wait()
    load_c[2].wait()
    work(1, g.at[1], g.at[3])
    when(s == 0, edge_before.start)
    when(s == slabs - 1, edge_after.start)
    to_right.wait_recv()
    to_left.wait_recv()
    pl.semaphore_signal(y_ok, inc=1, device_id=(q_to, s), device_id_type=MESH)
    pl.semaphore_signal(q_ok, inc=1, device_id=(y_to, s), device_id_type=MESH)
    pl.semaphore_wait(y_ok, 1)
    pl.semaphore_wait(q_ok, 1)
    when(late, lambda: loop(per, 2 * per, lambda t: y_copy(t).start()))
    when(early, lambda: loop(0, 3, forward))
    load_c[0].wait()
    work(2, before, g.at[1])
    load_c[3].wait()
    work(3, g.at[2], after)

    n = bose[0]
    has_up = e + 2 * OFF < energies
    has_down = e >= 2 * OFF
    y_own = jnp.where(upper == 0, n, n + 1.0)
    y_far = jnp.where(upper == 0, jnp.where(has_up, n + 1.0, 0.0), jnp.where(has_down, n, 0.0))
    q_own = jnp.where(upper == 0, n + 1.0, n)
    q_far = jnp.where(upper == 0, jnp.where(has_down, n, 0.0), jnp.where(has_up, n + 1.0, 0.0))

    def combine(own, far, own_factor, far_factor, cnt, block):
        active = cnt[0:1, :] > block
        total = own_factor * own.astype(jnp.float32) + far_factor * far.astype(jnp.float32)
        return jnp.where(active, total, 0.0).astype(jnp.bfloat16)

    def across(t):
        j, r = rows_of(t)
        y_copy(t).wait_recv()
        sig[j, r, :] = combine(part[j, r, :], got_y[j, r, :], y_own, y_far, cnt_got, s * 4 + block_of(j))
        o_copy(t).start()

    count.wait_recv()
    period = 2 * per

    def early_part():
        loop(3, 8, forward)
        loop(8, 10, across)
        loop(12, 14, forward)
        loop(10, 12, across)
        loop(14, 16, forward)

    def late_part():
        loop(0, 2, forward)
        loop(2, 4, lambda t: (across(t + 2), forward(t)))
        loop(6, 16, across)

    when(early, early_part)
    when(late, late_part)

    def own(t):
        def action():
            j, r = rows_of(t)
            q_copy(t).wait_recv()
            sigma[0, block_of(j), r, :] = combine(
                got_z[j, r, :], got_q[j, r, :], q_own, q_far, cnt_own, s * 4 + block_of(j)
            )

        when(z_first(t), action)

    loop(0, 2 * period, own)

    when(s < slabs - 1, to_right.wait_send)
    when(s > 0, to_left.wait_send)
    count.wait_send()

    def finish(t):
        def z_way():
            z_copy(t).wait_send()
            q_copy(t).wait_send()

        def y_way():
            y_copy(t).wait_send()
            o_copy(t).wait_send()
            o_copy(t).wait_recv()

        when(z_first(t), z_way)
        when(jnp.logical_not(z_first(t)), y_way)

    loop(0, 2 * period, finish)


def solution(mesh):
    energies, slabs = mesh.shape["energy"], mesh.shape["slab"]

    def on_device(green, coupling, bonds, counts, bose):
        orb = green.shape[-1]
        tiles = 4 * (orb // ROWS)
        block = (orb, orb)
        dma = pltpu.SemaphoreType.DMA
        whole = pltpu.VMEM((4,) + block, jnp.bfloat16)
        hbm = pl.BlockSpec(memory_space=pltpu.HBM)
        return pl.pallas_call(
            functools.partial(kernel, energies, slabs),
            out_shape=pltpu.VMEM(green.shape, jnp.bfloat16),
            in_specs=[hbm] * 5,
            out_specs=pl.BlockSpec(memory_space=pltpu.VMEM),
            scratch_shapes=[
                whole,
                pltpu.VMEM(block, jnp.bfloat16),
                pltpu.VMEM(block, jnp.bfloat16),
            ]
            + [pltpu.VMEM((3,) + block, jnp.bfloat16)] * 4
            + [whole] * 5
            + [pltpu.VMEM((8, orb), jnp.int32)] * 2
            + [pltpu.SMEM(bonds.shape, jnp.int32), pltpu.SMEM((1,), jnp.int32), pltpu.SMEM((1,), jnp.float32)]
            + [dma((8,)), dma((3,)), dma((2,)), dma((2,)), dma((2,))] + [pltpu.SemaphoreType.REGULAR] * 2
            + [dma((tiles,))] * 8,
            compiler_params=pltpu.CompilerParams(
                collective_id=0, has_side_effects=True, vmem_limit_bytes=60 * MIB
            ),
            cost_estimate=pl.CostEstimate(
                flops=48 * orb**3, bytes_accessed=20 * MIB, transcendentals=0
            ),
            name="self_energy",
        )(green, coupling, bonds, counts, bose)

    return jax.shard_map(
        on_device,
        mesh=mesh,
        in_specs=(
            P("energy", "slab", None, None),
            P("slab", None, None, None),
            P("slab", None),
            P("energy"),
            P(),
        ),
        out_specs=P("energy", "slab", None, None),
        check_vma=False,
    )
```

```python
import functools

import jax
import jax.numpy as jnp
from jax import lax
from jax.experimental import pallas as pl
from jax.experimental.pallas import tpu as pltpu
from jax.sharding import PartitionSpec as P

OFF = 8
ROWS = 128
MESH = pl.DeviceIdType.MESH
MIB = 2**20
ORDER = (1, 2, 0, 3)


def kernel(
    energies, slabs,
    green, coupling, bonds_hbm, counts_hbm, bose_hbm, sigma,
    g, before, after, c0, c1, c2, c3,
    part, got_z, got_q, got_y, sig, cnt_own, cnt_got, bonds, counts, bose,
    load_sem, small_sem, halo_send, halo_recv, cnt_sem, y_ok, q_ok,
    z_send, z_recv, q_send, q_recv, y_send, y_recv, o_send, o_recv,
):
    e = lax.axis_index("energy")
    s = lax.axis_index("slab")
    orb = g.shape[-1]
    per = orb // ROWS
    upper = (e // OFF) % 2
    late = (e // 4) % 2 == 1
    early = jnp.logical_not(late)
    partner = e + OFF - 2 * OFF * upper
    up = (e + 2 * OFF) % energies
    down = (e + energies - 2 * OFF) % energies
    y_to = jnp.where(upper == 0, down, up)
    q_to = jnp.where(upper == 0, up, down)
    left = (s + slabs - 1) % slabs
    right = (s + 1) % slabs

    has_up = e + 2 * OFF < energies
    has_down = e >= 2 * OFF
    has_left = s > 0
    has_right = s < slabs - 1
    y_in = jnp.where(upper == 0, has_up, has_down)
    y_out = jnp.where(upper == 0, has_down, has_up)
    q_in, q_out = y_out, y_in

    def when(flag, action):
        @pl.when(flag)
        def _():
            action()

    def signal(semaphore, device):
        pl.semaphore_signal(semaphore, inc=1, device_id=device, device_id_type=MESH)

    barrier = pltpu.get_barrier_semaphore()
    signal(barrier, (partner, s))
    for flag, device in (
        (has_up, (up, s)), (has_down, (down, s)), (has_left, (e, left)), (has_right, (e, right)),
    ):
        when(flag, lambda device=device: signal(barrier, device))
    n_peers = 1 + sum(flag.astype(jnp.int32) for flag in (has_up, has_down, has_left, has_right))

    blocks = (c0, c1, c2, c3)
    small = [
        pltpu.make_async_copy(src, dst, small_sem.at[i])
        for i, (src, dst) in enumerate(((bonds_hbm, bonds), (counts_hbm, counts), (bose_hbm, bose)))
    ]
    for copy in small:
        copy.start()
    load_g = [pltpu.make_async_copy(green.at[0, b], g.at[b], load_sem.at[b]) for b in range(4)]
    load_c = [pltpu.make_async_copy(coupling.at[b], blocks[b], load_sem.at[4 + b]) for b in range(4)]
    for copy in (load_g[1], load_c[1], load_g[0], load_g[2]):
        copy.start()
    for copy in small:
        copy.wait()
    cnt_own[...] = jnp.full(cnt_own.shape, counts[0], jnp.int32)

    def remote(src, dst, send, recv, device):
        return pltpu.make_async_remote_copy(
            src_ref=src, dst_ref=dst, send_sem=send, recv_sem=recv,
            device_id=device, device_id_type=MESH,
        )

    to_right = remote(green.at[0, 3], before, halo_send.at[0], halo_recv.at[0], (e, right))
    to_left = remote(green.at[0, 0], after, halo_send.at[1], halo_recv.at[1], (e, left))
    edge_before = pltpu.make_async_copy(green.at[0, 1], before, halo_recv.at[0])
    edge_after = pltpu.make_async_copy(green.at[0, 2], after, halo_recv.at[1])
    count = remote(cnt_own, cnt_got, cnt_sem.at[0], cnt_sem.at[1], (partner, s))

    def rows_of(t):
        return t // per, pl.ds(pl.multiple_of((t % per) * ROWS, ROWS), ROWS)

    def block_of(j):
        return jnp.where(j < 2, j + 1, jnp.where(j == 2, 0, 3))

    def z_copy(t):
        j, r = rows_of(t)
        return remote(part.at[j, r], got_z.at[j, r], z_send.at[t], z_recv.at[t], (partner, s))

    def q_copy(t):
        j, r = rows_of(t)
        return remote(got_z.at[j, r], got_q.at[j, r], q_send.at[t], q_recv.at[t], (q_to, s))

    def y_copy(t):
        j, r = rows_of(t)
        return remote(part.at[j, r], got_y.at[j, r], y_send.at[t], y_recv.at[t], (y_to, s))

    def o_copy(t):
        j, r = rows_of(t)
        return remote(sig.at[j, r], sigma.at[0, block_of(j), r], o_send.at[t], o_recv.at[t], (partner, s))

    def z_first(t):
        return jnp.where(early, t // per != 2, t // per == 0)

    def loop(first, last, body):
        def step(t, _):
            body(t)
            return 0

        lax.fori_loop(first, last, step, 0)

    def products(b, r, lower, higher):
        c = blocks[b]
        k = 1 + (bonds[b, 1] > bonds[b, 0]).astype(jnp.int32)
        total = None
        for k, near in ((0, g.at[b]), (k, lower), (3 - k, higher)):
            half = jnp.dot(c[k, r, :], near[...], preferred_element_type=jnp.float32)
            term = lax.dot_general(
                half.astype(jnp.bfloat16), c[k], (((1,), (1,)), ((), ())),
                preferred_element_type=jnp.float32,
            )
            total = term if total is None else total + term
        return total.astype(jnp.bfloat16)

    def first_sends():
        pl.semaphore_wait(barrier, n_peers)
        when(has_right, to_right.start)
        when(has_left, to_left.start)
        count.start()

    def work(j, lower, higher):
        def tile(t):
            _, r = rows_of(t)
            part[j, r, :] = products(ORDER[j], r, lower, higher)
            if j == 0:
                when(t == 0, first_sends)
            if j == 0:
                z_copy(t).start()
            elif j == 2:
                when(y_out, y_copy(t).start)
            else:
                when(early, z_copy(t).start)
                if j == 3:
                    when(jnp.logical_and(late, y_out), y_copy(t).start)

        loop(j * per, (j + 1) * per, tile)

    def forward(t):
        z_copy(t).wait_recv()
        when(q_out, q_copy(t).start)

    for b in (1, 0, 2):
        load_g[b].wait()
    load_c[1].wait()
    for copy in (load_c[2], load_g[3], load_c[0], load_c[3]):
        copy.start()
    work(0, g.at[0], g.at[2])
    load_g[3].wait()
    load_c[2].wait()
    work(1, g.at[1], g.at[3])
    when(s == 0, edge_before.start)
    when(s == slabs - 1, edge_after.start)
    to_right.wait_recv()
    to_left.wait_recv()
    when(y_in, lambda: signal(y_ok, (q_to, s)))
    when(q_in, lambda: signal(q_ok, (y_to, s)))
    when(y_out, lambda: pl.semaphore_wait(y_ok, 1))
    when(q_out, lambda: pl.semaphore_wait(q_ok, 1))
    when(jnp.logical_and(late, y_out), lambda: loop(per, 2 * per, lambda t: y_copy(t).start()))
    when(early, lambda: loop(0, 3, forward))
    load_c[0].wait()
    work(2, before, g.at[1])
    load_c[3].wait()
    work(3, g.at[2], after)

    n = bose[0]
    y_own, y_far = jnp.where(upper == 0, n, n + 1.0), jnp.where(upper == 0, n + 1.0, n)
    q_own, q_far = y_far, y_own

    def combine(target, terms, cnt, block):
        total = sum(factor * value.astype(jnp.float32) for factor, value in terms)
        target[...] = jnp.where(cnt[0:1, :] > block, total, 0.0).astype(jnp.bfloat16)

    def across(t):
        j, r = rows_of(t)
        own = (y_own, part[j, r, :])
        block = s * 4 + block_of(j)

        def both():
            y_copy(t).wait_recv()
            combine(sig.at[j, r], (own, (y_far, got_y[j, r, :])), cnt_got, block)

        when(y_in, both)
        when(jnp.logical_not(y_in), lambda: combine(sig.at[j, r], (own,), cnt_got, block))
        o_copy(t).start()

    count.wait_recv()
    period = 2 * per

    def early_part():
        loop(3, 8, forward)
        loop(8, 10, across)
        loop(12, 14, forward)
        loop(10, 12, across)
        loop(14, 16, forward)

    def late_part():
        loop(0, 2, forward)
        loop(2, 4, lambda t: (across(t + 2), forward(t)))
        loop(6, 16, across)

    when(early, early_part)
    when(late, late_part)

    def keep(t):
        j, r = rows_of(t)
        target = sigma.at[0, block_of(j), r]
        block = s * 4 + block_of(j)

        def both():
            q_copy(t).wait_recv()
            combine(target, ((q_own, got_z[j, r, :]), (q_far, got_q[j, r, :])), cnt_own, block)

        when(q_in, both)
        when(jnp.logical_not(q_in), lambda: combine(target, ((q_own, got_z[j, r, :]),), cnt_own, block))

    loop(0, 2 * period, lambda t: when(z_first(t), lambda: keep(t)))

    when(has_right, to_right.wait_send)
    when(has_left, to_left.wait_send)
    count.wait_send()

    def finish(t):
        def z_way():
            z_copy(t).wait_send()
            when(q_out, q_copy(t).wait_send)

        def y_way():
            when(y_out, y_copy(t).wait_send)
            o_copy(t).wait_send()
            o_copy(t).wait_recv()

        when(z_first(t), z_way)
        when(jnp.logical_not(z_first(t)), y_way)

    loop(0, 2 * period, finish)


def solution(mesh):
    energies, slabs = mesh.shape["energy"], mesh.shape["slab"]

    def on_device(green, coupling, bonds, counts, bose):
        orb = green.shape[-1]
        tiles = 4 * (orb // ROWS)
        block = (orb, orb)
        dma = pltpu.SemaphoreType.DMA
        whole = pltpu.VMEM((4,) + block, jnp.bfloat16)
        hbm = pl.BlockSpec(memory_space=pltpu.HBM)
        return pl.pallas_call(
            functools.partial(kernel, energies, slabs),
            out_shape=pltpu.VMEM(green.shape, jnp.bfloat16),
            in_specs=[hbm] * 5,
            out_specs=pl.BlockSpec(memory_space=pltpu.VMEM),
            scratch_shapes=[
                whole,
                pltpu.VMEM(block, jnp.bfloat16),
                pltpu.VMEM(block, jnp.bfloat16),
            ]
            + [pltpu.VMEM((3,) + block, jnp.bfloat16)] * 4
            + [whole] * 5
            + [pltpu.VMEM((8, orb), jnp.int32)] * 2
            + [pltpu.SMEM(bonds.shape, jnp.int32), pltpu.SMEM((1,), jnp.int32), pltpu.SMEM((1,), jnp.float32)]
            + [dma((8,)), dma((3,)), dma((2,)), dma((2,)), dma((2,))] + [pltpu.SemaphoreType.REGULAR] * 2
            + [dma((tiles,))] * 8,
            compiler_params=pltpu.CompilerParams(
                collective_id=0, has_side_effects=True, vmem_limit_bytes=60 * MIB
            ),
            cost_estimate=pl.CostEstimate(
                flops=48 * orb**3, bytes_accessed=20 * MIB, transcendentals=0
            ),
            name="self_energy",
        )(green, coupling, bonds, counts, bose)

    return jax.shard_map(
        on_device,
        mesh=mesh,
        in_specs=(
            P("energy", "slab", None, None),
            P("slab", None, None, None),
            P("slab", None),
            P("energy"),
            P(),
        ),
        out_specs=P("energy", "slab", None, None),
        check_vma=False,
    )
```

```python
import functools

import jax
import jax.numpy as jnp
from jax import lax
from jax.experimental import pallas as pl
from jax.experimental.pallas import tpu as pltpu
from jax.sharding import PartitionSpec as P

OFF = 8
ROWS = 128
MESH = pl.DeviceIdType.MESH
MIB = 2**20
ORDER = (1, 2, 0, 3)
CHUNK = (256, 512, 512, 512)


def kernel(
    energies, slabs,
    green, coupling, bonds_hbm, counts_hbm, bose_hbm, sigma,
    g, before, after, c0, c1, c2, c3,
    part, got_z, got_q, got_y, sig, cnt_own, cnt_got, bonds, counts, bose,
    load_sem, small_sem, halo_send, halo_recv, cnt_sem, y_ok, q_ok,
    z_send, z_recv, q_send, q_recv, y_send, y_recv, o_send, o_recv,
):
    e = lax.axis_index("energy")
    s = lax.axis_index("slab")
    orb = g.shape[-1]
    per = orb // ROWS
    upper = (e // OFF) % 2
    late = (e // 4) % 2 == 1
    early = jnp.logical_not(late)
    partner = e + OFF - 2 * OFF * upper
    up = (e + 2 * OFF) % energies
    down = (e + energies - 2 * OFF) % energies
    y_to = jnp.where(upper == 0, down, up)
    q_to = jnp.where(upper == 0, up, down)
    left = (s + slabs - 1) % slabs
    right = (s + 1) % slabs

    has_up = e + 2 * OFF < energies
    has_down = e >= 2 * OFF
    has_left = s > 0
    has_right = s < slabs - 1
    y_in = jnp.where(upper == 0, has_up, has_down)
    y_out = jnp.where(upper == 0, has_down, has_up)
    q_in, q_out = y_out, y_in

    def when(flag, action):
        @pl.when(flag)
        def _():
            action()

    def signal(semaphore, device):
        pl.semaphore_signal(semaphore, inc=1, device_id=device, device_id_type=MESH)

    barrier = pltpu.get_barrier_semaphore()
    signal(barrier, (partner, s))
    for flag, device in (
        (has_up, (up, s)), (has_down, (down, s)), (has_left, (e, left)), (has_right, (e, right)),
    ):
        when(flag, lambda device=device: signal(barrier, device))
    n_peers = 1 + sum(flag.astype(jnp.int32) for flag in (has_up, has_down, has_left, has_right))

    blocks = (c0, c1, c2, c3)
    small = [
        pltpu.make_async_copy(src, dst, small_sem.at[i])
        for i, (src, dst) in enumerate(((bonds_hbm, bonds), (counts_hbm, counts), (bose_hbm, bose)))
    ]
    for copy in small:
        copy.start()
    load_g = [pltpu.make_async_copy(green.at[0, b], g.at[b], load_sem.at[b]) for b in range(4)]
    load_c = [pltpu.make_async_copy(coupling.at[b], blocks[b], load_sem.at[4 + b]) for b in range(4)]
    for copy in (load_g[1], load_c[1], load_g[0], load_g[2]):
        copy.start()
    for copy in small:
        copy.wait()
    cnt_own[...] = jnp.full(cnt_own.shape, counts[0], jnp.int32)

    def remote(src, dst, send, recv, device):
        return pltpu.make_async_remote_copy(
            src_ref=src, dst_ref=dst, send_sem=send, recv_sem=recv,
            device_id=device, device_id_type=MESH,
        )

    to_right = remote(green.at[0, 3], before, halo_send.at[0], halo_recv.at[0], (e, right))
    to_left = remote(green.at[0, 0], after, halo_send.at[1], halo_recv.at[1], (e, left))
    edge_before = pltpu.make_async_copy(green.at[0, 1], before, halo_recv.at[0])
    edge_after = pltpu.make_async_copy(green.at[0, 2], after, halo_recv.at[1])
    count = remote(cnt_own, cnt_got, cnt_sem.at[0], cnt_sem.at[1], (partner, s))

    def rows_of(t):
        return t // per, pl.ds(pl.multiple_of((t % per) * ROWS, ROWS), ROWS)

    def block_of(j):
        return jnp.where(j < 2, j + 1, jnp.where(j == 2, 0, 3))

    def z_copy(t):
        j, r = rows_of(t)
        return remote(part.at[j, r], got_z.at[j, r], z_send.at[t], z_recv.at[t], (partner, s))

    def q_copy(t):
        j, r = rows_of(t)
        return remote(got_z.at[j, r], got_q.at[j, r], q_send.at[t], q_recv.at[t], (q_to, s))

    def y_copy(t):
        j, r = rows_of(t)
        return remote(part.at[j, r], got_y.at[j, r], y_send.at[t], y_recv.at[t], (y_to, s))

    def o_copy(t):
        j, r = rows_of(t)
        return remote(sig.at[j, r], sigma.at[0, block_of(j), r], o_send.at[t], o_recv.at[t], (partner, s))

    def z_first(t):
        return jnp.where(early, t // per != 2, t // per == 0)

    def loop(first, last, body):
        def step(t, _):
            body(t)
            return 0

        lax.fori_loop(first, last, step, 0)

    def products(b, r, lower, higher):
        c = blocks[b]
        k = 1 + (bonds[b, 1] > bonds[b, 0]).astype(jnp.int32)
        total = None
        for k, near in ((0, g.at[b]), (k, lower), (3 - k, higher)):
            half = jnp.dot(c[k, r, :], near[...], preferred_element_type=jnp.float32)
            term = lax.dot_general(
                half.astype(jnp.bfloat16), c[k], (((1,), (1,)), ((), ())),
                preferred_element_type=jnp.float32,
            )
            total = term if total is None else total + term
        return total.astype(jnp.bfloat16)

    def first_sends():
        pl.semaphore_wait(barrier, n_peers)
        when(has_right, to_right.start)
        when(has_left, to_left.start)
        count.start()

    def work(j, lower, higher, send=None):
        rows = CHUNK[j]

        def chunk(i):
            r = pl.ds(pl.multiple_of(i * rows, rows), rows)
            part[j, r, :] = products(ORDER[j], r, lower, higher)
            if j == 0:
                when(i == 0, first_sends)
            if send is not None:
                first = j * per + i * (rows // ROWS)
                loop(first, first + rows // ROWS, send)

        loop(0, orb // rows, chunk)

    def forward(t):
        z_copy(t).wait_recv()
        when(q_out, q_copy(t).start)

    for b in (1, 0, 2):
        load_g[b].wait()
    load_c[1].wait()
    for copy in (load_c[2], load_g[3], load_c[0], load_c[3]):
        copy.start()
    work(0, g.at[0], g.at[2], lambda t: z_copy(t).start())
    load_g[3].wait()
    load_c[2].wait()
    work(1, g.at[1], g.at[3], lambda t: when(early, z_copy(t).start))
    when(s == 0, edge_before.start)
    when(s == slabs - 1, edge_after.start)
    to_right.wait_recv()
    to_left.wait_recv()
    when(y_in, lambda: signal(y_ok, (q_to, s)))
    when(q_in, lambda: signal(q_ok, (y_to, s)))
    load_c[0].wait()
    work(2, before, g.at[1])
    when(y_out, lambda: pl.semaphore_wait(y_ok, 1))
    when(q_out, lambda: pl.semaphore_wait(q_ok, 1))
    when(jnp.logical_and(late, y_out), lambda: loop(per, 2 * per, lambda t: y_copy(t).start()))
    when(y_out, lambda: loop(2 * per, 3 * per, lambda t: y_copy(t).start()))
    when(early, lambda: loop(0, 3, forward))
    load_c[3].wait()
    work(3, g.at[2], after, lambda t: (
        when(early, z_copy(t).start), when(jnp.logical_and(late, y_out), y_copy(t).start)
    ))

    n = bose[0]
    y_own, y_far = jnp.where(upper == 0, n, n + 1.0), jnp.where(upper == 0, n + 1.0, n)
    q_own, q_far = y_far, y_own

    def combine(target, terms, cnt, block):
        total = sum(factor * value.astype(jnp.float32) for factor, value in terms)
        target[...] = jnp.where(cnt[0:1, :] > block, total, 0.0).astype(jnp.bfloat16)

    def across(t):
        j, r = rows_of(t)
        own = (y_own, part[j, r, :])
        block = s * 4 + block_of(j)

        def both():
            y_copy(t).wait_recv()
            combine(sig.at[j, r], (own, (y_far, got_y[j, r, :])), cnt_got, block)

        when(y_in, both)
        when(jnp.logical_not(y_in), lambda: combine(sig.at[j, r], (own,), cnt_got, block))
        o_copy(t).start()

    count.wait_recv()
    period = 2 * per

    def early_part():
        loop(3, 8, forward)
        loop(8, 10, across)
        loop(12, 14, forward)
        loop(10, 12, across)
        loop(14, 16, forward)

    def late_part():
        loop(0, 2, forward)
        loop(2, 4, lambda t: (across(t + 2), forward(t)))
        loop(6, 16, across)

    when(early, early_part)
    when(late, late_part)

    def keep(t):
        j, r = rows_of(t)
        target = sigma.at[0, block_of(j), r]
        block = s * 4 + block_of(j)

        def both():
            q_copy(t).wait_recv()
            combine(target, ((q_own, got_z[j, r, :]), (q_far, got_q[j, r, :])), cnt_own, block)

        when(q_in, both)
        when(jnp.logical_not(q_in), lambda: combine(target, ((q_own, got_z[j, r, :]),), cnt_own, block))

    loop(0, 2 * period, lambda t: when(z_first(t), lambda: keep(t)))

    when(has_right, to_right.wait_send)
    when(has_left, to_left.wait_send)
    count.wait_send()

    def finish(t):
        def z_way():
            z_copy(t).wait_send()
            when(q_out, q_copy(t).wait_send)

        def y_way():
            when(y_out, y_copy(t).wait_send)
            o_copy(t).wait_send()
            o_copy(t).wait_recv()

        when(z_first(t), z_way)
        when(jnp.logical_not(z_first(t)), y_way)

    loop(0, 2 * period, finish)


def solution(mesh):
    energies, slabs = mesh.shape["energy"], mesh.shape["slab"]

    def on_device(green, coupling, bonds, counts, bose):
        orb = green.shape[-1]
        tiles = 4 * (orb // ROWS)
        block = (orb, orb)
        dma = pltpu.SemaphoreType.DMA
        whole = pltpu.VMEM((4,) + block, jnp.bfloat16)
        hbm = pl.BlockSpec(memory_space=pltpu.HBM)
        return pl.pallas_call(
            functools.partial(kernel, energies, slabs),
            out_shape=pltpu.VMEM(green.shape, jnp.bfloat16),
            in_specs=[hbm] * 5,
            out_specs=pl.BlockSpec(memory_space=pltpu.VMEM),
            scratch_shapes=[
                whole,
                pltpu.VMEM(block, jnp.bfloat16),
                pltpu.VMEM(block, jnp.bfloat16),
            ]
            + [pltpu.VMEM((3,) + block, jnp.bfloat16)] * 4
            + [whole] * 5
            + [pltpu.VMEM((8, orb), jnp.int32)] * 2
            + [pltpu.SMEM(bonds.shape, jnp.int32), pltpu.SMEM((1,), jnp.int32), pltpu.SMEM((1,), jnp.float32)]
            + [dma((8,)), dma((3,)), dma((2,)), dma((2,)), dma((2,))] + [pltpu.SemaphoreType.REGULAR] * 2
            + [dma((tiles,))] * 8,
            compiler_params=pltpu.CompilerParams(
                collective_id=0, has_side_effects=True, vmem_limit_bytes=60 * MIB
            ),
            cost_estimate=pl.CostEstimate(
                flops=48 * orb**3, bytes_accessed=20 * MIB, transcendentals=0
            ),
            name="self_energy",
        )(green, coupling, bonds, counts, bose)

    return jax.shard_map(
        on_device,
        mesh=mesh,
        in_specs=(
            P("energy", "slab", None, None),
            P("slab", None, None, None),
            P("slab", None),
            P("energy"),
            P(),
        ),
        out_specs=P("energy", "slab", None, None),
        check_vma=False,
    )
```

```python
import functools

import jax
import jax.numpy as jnp
from jax import lax
from jax.experimental import pallas as pl
from jax.experimental.pallas import tpu as pltpu
from jax.sharding import PartitionSpec as P

OFF = 8
ROWS = 128
MESH = pl.DeviceIdType.MESH
MIB = 2**20
ORDER = (1, 2, 0, 3)
CHUNK = (128, 512, 512, 512)


def kernel(
    energies, slabs,
    green, coupling, bonds_hbm, counts_hbm, bose_hbm, sigma,
    g, before, after, c0, c1, c2, c3,
    part, got_z, got_q, got_y, sig, cnt_own, cnt_got, bonds, counts, bose,
    load_sem, small_sem, halo_send, halo_recv, cnt_sem, y_ok, q_ok,
    z_send, z_recv, q_send, q_recv, y_send, y_recv, o_send, o_recv,
):
    e = lax.axis_index("energy")
    s = lax.axis_index("slab")
    orb = g.shape[-1]
    per = orb // ROWS
    upper = (e // OFF) % 2
    late = (e // 4) % 2 == 1
    early = jnp.logical_not(late)
    partner = e + OFF - 2 * OFF * upper
    up = (e + 2 * OFF) % energies
    down = (e + energies - 2 * OFF) % energies
    y_to = jnp.where(upper == 0, down, up)
    q_to = jnp.where(upper == 0, up, down)
    left = (s + slabs - 1) % slabs
    right = (s + 1) % slabs

    has_up = e + 2 * OFF < energies
    has_down = e >= 2 * OFF
    has_left = s > 0
    has_right = s < slabs - 1
    y_in = jnp.where(upper == 0, has_up, has_down)
    y_out = jnp.where(upper == 0, has_down, has_up)
    q_in, q_out = y_out, y_in

    def when(flag, action):
        @pl.when(flag)
        def _():
            action()

    def signal(semaphore, device):
        pl.semaphore_signal(semaphore, inc=1, device_id=device, device_id_type=MESH)

    barrier = pltpu.get_barrier_semaphore()
    signal(barrier, (partner, s))
    for flag, device in (
        (has_up, (up, s)), (has_down, (down, s)), (has_left, (e, left)), (has_right, (e, right)),
    ):
        when(flag, lambda device=device: signal(barrier, device))
    n_peers = 1 + sum(flag.astype(jnp.int32) for flag in (has_up, has_down, has_left, has_right))

    blocks = (c0, c1, c2, c3)
    small = [
        pltpu.make_async_copy(src, dst, small_sem.at[i])
        for i, (src, dst) in enumerate(((bonds_hbm, bonds), (counts_hbm, counts), (bose_hbm, bose)))
    ]
    for copy in small:
        copy.start()
    load_g = [pltpu.make_async_copy(green.at[0, b], g.at[b], load_sem.at[b]) for b in range(4)]
    load_c = [pltpu.make_async_copy(coupling.at[b], blocks[b], load_sem.at[4 + b]) for b in range(4)]
    for copy in (load_g[1], load_c[1], load_g[0], load_g[2]):
        copy.start()
    for copy in small:
        copy.wait()
    cnt_own[...] = jnp.full(cnt_own.shape, counts[0], jnp.int32)

    def remote(src, dst, send, recv, device):
        return pltpu.make_async_remote_copy(
            src_ref=src, dst_ref=dst, send_sem=send, recv_sem=recv,
            device_id=device, device_id_type=MESH,
        )

    to_right = remote(green.at[0, 3], before, halo_send.at[0], halo_recv.at[0], (e, right))
    to_left = remote(green.at[0, 0], after, halo_send.at[1], halo_recv.at[1], (e, left))
    edge_before = pltpu.make_async_copy(green.at[0, 1], before, halo_recv.at[0])
    edge_after = pltpu.make_async_copy(green.at[0, 2], after, halo_recv.at[1])
    count = remote(cnt_own, cnt_got, cnt_sem.at[0], cnt_sem.at[1], (partner, s))

    def rows_of(t):
        return t // per, pl.ds(pl.multiple_of((t % per) * ROWS, ROWS), ROWS)

    def block_of(j):
        return jnp.where(j < 2, j + 1, jnp.where(j == 2, 0, 3))

    def z_copy(t):
        j, r = rows_of(t)
        return remote(part.at[j, r], got_z.at[j, r], z_send.at[t], z_recv.at[t], (partner, s))

    def q_copy(t):
        j, r = rows_of(t)
        return remote(got_z.at[j, r], got_q.at[j, r], q_send.at[t], q_recv.at[t], (q_to, s))

    def y_copy(t):
        j, r = rows_of(t)
        return remote(part.at[j, r], got_y.at[j, r], y_send.at[t], y_recv.at[t], (y_to, s))

    def o_copy(t):
        j, r = rows_of(t)
        return remote(sig.at[j, r], sigma.at[0, block_of(j), r], o_send.at[t], o_recv.at[t], (partner, s))

    def z_first(t):
        return jnp.where(early, t // per != 2, t // per == 0)

    def loop(first, last, body):
        def step(t, _):
            body(t)
            return 0

        lax.fori_loop(first, last, step, 0)

    def products(b, r, lower, higher):
        c = blocks[b]
        k = 1 + (bonds[b, 1] > bonds[b, 0]).astype(jnp.int32)
        total = None
        for k, near in ((0, g.at[b]), (k, lower), (3 - k, higher)):
            half = jnp.dot(c[k, r, :], near[...], preferred_element_type=jnp.float32)
            term = lax.dot_general(
                half.astype(jnp.bfloat16), c[k], (((1,), (1,)), ((), ())),
                preferred_element_type=jnp.float32,
            )
            total = term if total is None else total + term
        return total.astype(jnp.bfloat16)

    def first_sends():
        pl.semaphore_wait(barrier, n_peers)
        when(has_right, to_right.start)
        when(has_left, to_left.start)
        count.start()

    def work(j, lower, higher, send=None):
        rows = CHUNK[j]

        def chunk(i):
            r = pl.ds(pl.multiple_of(i * rows, rows), rows)
            part[j, r, :] = products(ORDER[j], r, lower, higher)
            if j == 0:
                when(i == 0, first_sends)
            if send is not None:
                first = j * per + i * (rows // ROWS)
                loop(first, first + rows // ROWS, send)

        loop(0, orb // rows, chunk)

    def forward(t):
        z_copy(t).wait_recv()
        when(q_out, q_copy(t).start)

    for b in (1, 0, 2):
        load_g[b].wait()
    load_c[1].wait()
    for copy in (load_c[2], load_g[3], load_c[0], load_c[3]):
        copy.start()
    work(0, g.at[0], g.at[2], lambda t: z_copy(t).start())
    load_g[3].wait()
    load_c[2].wait()
    work(1, g.at[1], g.at[3], lambda t: when(early, z_copy(t).start))
    when(s == 0, edge_before.start)
    when(s == slabs - 1, edge_after.start)
    to_right.wait_recv()
    to_left.wait_recv()
    load_c[0].wait()
    work(2, before, g.at[1])
    when(y_in, lambda: signal(y_ok, (q_to, s)))
    when(q_in, lambda: signal(q_ok, (y_to, s)))
    load_c[3].wait()
    work(3, g.at[2], after, lambda t: when(early, z_copy(t).start))
    when(y_out, lambda: pl.semaphore_wait(y_ok, 1))
    when(q_out, lambda: pl.semaphore_wait(q_ok, 1))
    when(jnp.logical_and(late, y_out), lambda: loop(per, 4 * per, lambda t: y_copy(t).start()))
    when(jnp.logical_and(early, y_out), lambda: loop(2 * per, 3 * per, lambda t: y_copy(t).start()))
    when(early, lambda: loop(0, 3, forward))

    n = bose[0]
    y_own, y_far = jnp.where(upper == 0, n, n + 1.0), jnp.where(upper == 0, n + 1.0, n)
    q_own, q_far = y_far, y_own

    def combine(target, terms, cnt, block):
        total = sum(factor * value.astype(jnp.float32) for factor, value in terms)
        target[...] = jnp.where(cnt[0:1, :] > block, total, 0.0).astype(jnp.bfloat16)

    def across(t):
        j, r = rows_of(t)
        own = (y_own, part[j, r, :])
        block = s * 4 + block_of(j)

        def both():
            y_copy(t).wait_recv()
            combine(sig.at[j, r], (own, (y_far, got_y[j, r, :])), cnt_got, block)

        when(y_in, both)
        when(jnp.logical_not(y_in), lambda: combine(sig.at[j, r], (own,), cnt_got, block))
        o_copy(t).start()

    count.wait_recv()
    period = 2 * per

    def early_part():
        loop(3, 8, forward)
        loop(8, 10, across)
        loop(12, 14, forward)
        loop(10, 12, across)
        loop(14, 16, forward)

    def late_part():
        loop(0, 2, forward)
        loop(2, 4, lambda t: (across(t + 2), forward(t)))
        loop(6, 16, across)

    when(early, early_part)
    when(late, late_part)

    def keep(t):
        j, r = rows_of(t)
        target = sigma.at[0, block_of(j), r]
        block = s * 4 + block_of(j)

        def both():
            q_copy(t).wait_recv()
            combine(target, ((q_own, got_z[j, r, :]), (q_far, got_q[j, r, :])), cnt_own, block)

        when(q_in, both)
        when(jnp.logical_not(q_in), lambda: combine(target, ((q_own, got_z[j, r, :]),), cnt_own, block))

    loop(0, 2 * period, lambda t: when(z_first(t), lambda: keep(t)))

    when(has_right, to_right.wait_send)
    when(has_left, to_left.wait_send)
    count.wait_send()

    def finish(t):
        def z_way():
            z_copy(t).wait_send()
            when(q_out, q_copy(t).wait_send)

        def y_way():
            when(y_out, y_copy(t).wait_send)
            o_copy(t).wait_send()
            o_copy(t).wait_recv()

        when(z_first(t), z_way)
        when(jnp.logical_not(z_first(t)), y_way)

    loop(0, 2 * period, finish)


def solution(mesh):
    energies, slabs = mesh.shape["energy"], mesh.shape["slab"]

    def on_device(green, coupling, bonds, counts, bose):
        orb = green.shape[-1]
        tiles = 4 * (orb // ROWS)
        block = (orb, orb)
        dma = pltpu.SemaphoreType.DMA
        whole = pltpu.VMEM((4,) + block, jnp.bfloat16)
        hbm = pl.BlockSpec(memory_space=pltpu.HBM)
        return pl.pallas_call(
            functools.partial(kernel, energies, slabs),
            out_shape=pltpu.VMEM(green.shape, jnp.bfloat16),
            in_specs=[hbm] * 5,
            out_specs=pl.BlockSpec(memory_space=pltpu.VMEM),
            scratch_shapes=[
                whole,
                pltpu.VMEM(block, jnp.bfloat16),
                pltpu.VMEM(block, jnp.bfloat16),
            ]
            + [pltpu.VMEM((3,) + block, jnp.bfloat16)] * 4
            + [whole] * 5
            + [pltpu.VMEM((8, orb), jnp.int32)] * 2
            + [pltpu.SMEM(bonds.shape, jnp.int32), pltpu.SMEM((1,), jnp.int32), pltpu.SMEM((1,), jnp.float32)]
            + [dma((8,)), dma((3,)), dma((2,)), dma((2,)), dma((2,))] + [pltpu.SemaphoreType.REGULAR] * 2
            + [dma((tiles,))] * 8,
            compiler_params=pltpu.CompilerParams(
                collective_id=0, has_side_effects=True, vmem_limit_bytes=60 * MIB
            ),
            cost_estimate=pl.CostEstimate(
                flops=48 * orb**3, bytes_accessed=20 * MIB, transcendentals=0
            ),
            name="self_energy",
        )(green, coupling, bonds, counts, bose)

    return jax.shard_map(
        on_device,
        mesh=mesh,
        in_specs=(
            P("energy", "slab", None, None),
            P("slab", None, None, None),
            P("slab", None),
            P("energy"),
            P(),
        ),
        out_specs=P("energy", "slab", None, None),
        check_vma=False,
    )
```

```python
import functools

import jax
import jax.numpy as jnp
from jax import lax
from jax.experimental import pallas as pl
from jax.experimental.pallas import tpu as pltpu
from jax.sharding import PartitionSpec as P

OFF = 8
ROWS = 128
MESH = pl.DeviceIdType.MESH
MIB = 2**20
ORDER = (1, 2, 0, 3)
CHUNK = (128, 512, 512, 512)


def kernel(
    energies, slabs,
    green, coupling, bonds_hbm, counts_hbm, bose_hbm, sigma,
    g, before, after, c0, c1, c2, c3,
    part, got_z, got_q, got_y, sig, cnt_own, cnt_got, bonds, counts, bose,
    load_sem, small_sem, halo_send, halo_recv, cnt_sem, y_ok, q_ok,
    z_send, z_recv, q_send, q_recv, y_send, y_recv, o_send, o_recv,
):
    e = lax.axis_index("energy")
    s = lax.axis_index("slab")
    orb = g.shape[-1]
    per = orb // ROWS
    upper = (e // OFF) % 2
    late = (e // 4) % 2 == 1
    early = jnp.logical_not(late)
    partner = e + OFF - 2 * OFF * upper
    up = (e + 2 * OFF) % energies
    down = (e + energies - 2 * OFF) % energies
    y_to = jnp.where(upper == 0, down, up)
    q_to = jnp.where(upper == 0, up, down)
    left = (s + slabs - 1) % slabs
    right = (s + 1) % slabs

    has_up = e + 2 * OFF < energies
    has_down = e >= 2 * OFF
    has_left = s > 0
    has_right = s < slabs - 1
    y_in = jnp.where(upper == 0, has_up, has_down)
    y_out = jnp.where(upper == 0, has_down, has_up)
    q_in, q_out = y_out, y_in

    def when(flag, action):
        @pl.when(flag)
        def _():
            action()

    def signal(semaphore, device):
        pl.semaphore_signal(semaphore, inc=1, device_id=device, device_id_type=MESH)

    barrier = pltpu.get_barrier_semaphore()
    signal(barrier, (partner, s))
    for flag, device in (
        (has_up, (up, s)), (has_down, (down, s)), (has_left, (e, left)), (has_right, (e, right)),
    ):
        when(flag, lambda device=device: signal(barrier, device))
    n_peers = 1 + sum(flag.astype(jnp.int32) for flag in (has_up, has_down, has_left, has_right))

    blocks = (c0, c1, c2, c3)
    small = [
        pltpu.make_async_copy(src, dst, small_sem.at[i])
        for i, (src, dst) in enumerate(((bonds_hbm, bonds), (counts_hbm, counts), (bose_hbm, bose)))
    ]
    for copy in small:
        copy.start()
    load_g = [pltpu.make_async_copy(green.at[0, b], g.at[b], load_sem.at[b]) for b in range(4)]
    load_c = [pltpu.make_async_copy(coupling.at[b], blocks[b], load_sem.at[4 + b]) for b in range(4)]
    for copy in (load_g[1], load_c[1], load_g[0], load_g[2]):
        copy.start()
    for copy in small:
        copy.wait()
    cnt_own[...] = jnp.full(cnt_own.shape, counts[0], jnp.int32)

    def remote(src, dst, send, recv, device):
        return pltpu.make_async_remote_copy(
            src_ref=src, dst_ref=dst, send_sem=send, recv_sem=recv,
            device_id=device, device_id_type=MESH,
        )

    to_right = remote(green.at[0, 3], before, halo_send.at[0], halo_recv.at[0], (e, right))
    to_left = remote(green.at[0, 0], after, halo_send.at[1], halo_recv.at[1], (e, left))
    edge_before = pltpu.make_async_copy(green.at[0, 1], before, halo_recv.at[0])
    edge_after = pltpu.make_async_copy(green.at[0, 2], after, halo_recv.at[1])
    count = remote(cnt_own, cnt_got, cnt_sem.at[0], cnt_sem.at[1], (partner, s))

    def rows_of(t):
        return t // per, pl.ds(pl.multiple_of((t % per) * ROWS, ROWS), ROWS)

    def block_of(j):
        return jnp.where(j < 2, j + 1, jnp.where(j == 2, 0, 3))

    def z_copy(t):
        j, r = rows_of(t)
        return remote(part.at[j, r], got_z.at[j, r], z_send.at[t], z_recv.at[t], (partner, s))

    def q_copy(t):
        j, r = rows_of(t)
        return remote(got_z.at[j, r], got_q.at[j, r], q_send.at[t], q_recv.at[t], (q_to, s))

    def y_copy(t):
        j, r = rows_of(t)
        return remote(part.at[j, r], got_y.at[j, r], y_send.at[t], y_recv.at[t], (y_to, s))

    def o_copy(t):
        j, r = rows_of(t)
        return remote(sig.at[j, r], sigma.at[0, block_of(j), r], o_send.at[t], o_recv.at[t], (partner, s))

    def z_first(t):
        return jnp.where(early, t // per != 2, t // per == 0)

    def loop(first, last, body):
        def step(t, _):
            body(t)
            return 0

        lax.fori_loop(first, last, step, 0)

    def products(b, r, lower, higher):
        c = blocks[b]
        k = 1 + (bonds[b, 1] > bonds[b, 0]).astype(jnp.int32)
        total = None
        for k, near in ((0, g.at[b]), (k, lower), (3 - k, higher)):
            half = jnp.dot(c[k, r, :], near[...], preferred_element_type=jnp.float32)
            term = lax.dot_general(
                half.astype(jnp.bfloat16), c[k], (((1,), (1,)), ((), ())),
                preferred_element_type=jnp.float32,
            )
            total = term if total is None else total + term
        return total.astype(jnp.bfloat16)

    def first_sends():
        pl.semaphore_wait(barrier, n_peers)
        when(has_right, to_right.start)
        when(has_left, to_left.start)
        count.start()

    def work(j, lower, higher, send=None):
        rows = CHUNK[j]

        def chunk(i):
            r = pl.ds(pl.multiple_of(i * rows, rows), rows)
            part[j, r, :] = products(ORDER[j], r, lower, higher)
            if j == 0:
                when(i == 0, first_sends)
            if send is not None:
                first = j * per + i * (rows // ROWS)
                loop(first, first + rows // ROWS, send)

        loop(0, orb // rows, chunk)

    def forward(t):
        z_copy(t).wait_recv()
        when(q_out, q_copy(t).start)

    for b in (1, 0, 2):
        load_g[b].wait()
    load_c[1].wait()
    for copy in (load_c[2], load_g[3], load_c[0], load_c[3]):
        copy.start()
    work(0, g.at[0], g.at[2], lambda t: z_copy(t).start())
    load_g[3].wait()
    load_c[2].wait()
    work(1, g.at[1], g.at[3], lambda t: when(early, z_copy(t).start))
    when(s == 0, edge_before.start)
    when(s == slabs - 1, edge_after.start)
    to_right.wait_recv()
    to_left.wait_recv()
    when(y_in, lambda: signal(y_ok, (q_to, s)))
    when(q_in, lambda: signal(q_ok, (y_to, s)))
    load_c[0].wait()
    work(2, before, g.at[1])
    when(y_out, lambda: pl.semaphore_wait(y_ok, 1))
    when(q_out, lambda: pl.semaphore_wait(q_ok, 1))
    when(jnp.logical_and(late, y_out), lambda: loop(per, 2 * per, lambda t: y_copy(t).start()))
    when(y_out, lambda: loop(2 * per, 3 * per, lambda t: y_copy(t).start()))
    load_c[3].wait()
    work(3, g.at[2], after, lambda t: (
        when(early, z_copy(t).start), when(jnp.logical_and(late, y_out), y_copy(t).start)
    ))

    n = bose[0]
    y_own, y_far = jnp.where(upper == 0, n, n + 1.0), jnp.where(upper == 0, n + 1.0, n)
    q_own, q_far = y_far, y_own

    def combine(target, terms, cnt, block):
        total = sum(factor * value.astype(jnp.float32) for factor, value in terms)
        target[...] = jnp.where(cnt[0:1, :] > block, total, 0.0).astype(jnp.bfloat16)

    def across(t):
        j, r = rows_of(t)
        own = (y_own, part[j, r, :])
        block = s * 4 + block_of(j)

        def both():
            y_copy(t).wait_recv()
            combine(sig.at[j, r], (own, (y_far, got_y[j, r, :])), cnt_got, block)

        when(y_in, both)
        when(jnp.logical_not(y_in), lambda: combine(sig.at[j, r], (own,), cnt_got, block))
        o_copy(t).start()

    count.wait_recv()
    period = 2 * per

    def early_part():
        loop(0, 6, forward)
        loop(8, 10, across)
        loop(6, 8, forward)
        loop(10, 12, across)
        loop(12, 16, forward)

    def late_part():
        loop(4, 8, across)
        loop(0, 4, forward)
        loop(8, 16, across)

    when(early, early_part)
    when(late, late_part)

    def keep(t):
        j, r = rows_of(t)
        target = sigma.at[0, block_of(j), r]
        block = s * 4 + block_of(j)

        def both():
            q_copy(t).wait_recv()
            combine(target, ((q_own, got_z[j, r, :]), (q_far, got_q[j, r, :])), cnt_own, block)

        when(q_in, both)
        when(jnp.logical_not(q_in), lambda: combine(target, ((q_own, got_z[j, r, :]),), cnt_own, block))

    loop(0, 2 * period, lambda t: when(z_first(t), lambda: keep(t)))

    when(has_right, to_right.wait_send)
    when(has_left, to_left.wait_send)
    count.wait_send()

    def finish(t):
        def z_way():
            z_copy(t).wait_send()
            when(q_out, q_copy(t).wait_send)

        def y_way():
            when(y_out, y_copy(t).wait_send)
            o_copy(t).wait_send()
            o_copy(t).wait_recv()

        when(z_first(t), z_way)
        when(jnp.logical_not(z_first(t)), y_way)

    loop(0, 2 * period, finish)


def solution(mesh):
    energies, slabs = mesh.shape["energy"], mesh.shape["slab"]

    def on_device(green, coupling, bonds, counts, bose):
        orb = green.shape[-1]
        tiles = 4 * (orb // ROWS)
        block = (orb, orb)
        dma = pltpu.SemaphoreType.DMA
        whole = pltpu.VMEM((4,) + block, jnp.bfloat16)
        hbm = pl.BlockSpec(memory_space=pltpu.HBM)
        return pl.pallas_call(
            functools.partial(kernel, energies, slabs),
            out_shape=pltpu.VMEM(green.shape, jnp.bfloat16),
            in_specs=[hbm] * 5,
            out_specs=pl.BlockSpec(memory_space=pltpu.VMEM),
            scratch_shapes=[
                whole,
                pltpu.VMEM(block, jnp.bfloat16),
                pltpu.VMEM(block, jnp.bfloat16),
            ]
            + [pltpu.VMEM((3,) + block, jnp.bfloat16)] * 4
            + [whole] * 5
            + [pltpu.VMEM((8, orb), jnp.int32)] * 2
            + [pltpu.SMEM(bonds.shape, jnp.int32), pltpu.SMEM((1,), jnp.int32), pltpu.SMEM((1,), jnp.float32)]
            + [dma((8,)), dma((3,)), dma((2,)), dma((2,)), dma((2,))] + [pltpu.SemaphoreType.REGULAR] * 2
            + [dma((tiles,))] * 8,
            compiler_params=pltpu.CompilerParams(
                collective_id=0, has_side_effects=True, vmem_limit_bytes=60 * MIB
            ),
            cost_estimate=pl.CostEstimate(
                flops=48 * orb**3, bytes_accessed=20 * MIB, transcendentals=0
            ),
            name="self_energy",
        )(green, coupling, bonds, counts, bose)

    return jax.shard_map(
        on_device,
        mesh=mesh,
        in_specs=(
            P("energy", "slab", None, None),
            P("slab", None, None, None),
            P("slab", None),
            P("energy"),
            P(),
        ),
        out_specs=P("energy", "slab", None, None),
        check_vma=False,
    )
```

```python
import functools

import jax
import jax.numpy as jnp
from jax import lax
from jax.experimental import pallas as pl
from jax.experimental.pallas import tpu as pltpu
from jax.sharding import PartitionSpec as P

OFF = 8
ROWS = 128
MESH = pl.DeviceIdType.MESH
MIB = 2**20
ORDER = (1, 2, 0, 3)
CHUNK = (128, 512, 512, 512)


def kernel(
    energies, slabs,
    green, coupling, bonds_hbm, counts_hbm, bose_hbm, sigma,
    g, before, after, c0, c1, c2, c3,
    part, got_z, got_q, got_y, sig, cnt_own, cnt_got, bonds, counts, bose,
    load_sem, first_sem, small_sem, halo_send, halo_recv, cnt_sem, y_ok, q_ok,
    z_send, z_recv, q_send, q_recv, y_send, y_recv, o_send, o_recv,
):
    e = lax.axis_index("energy")
    s = lax.axis_index("slab")
    orb = g.shape[-1]
    per = orb // ROWS
    upper = (e // OFF) % 2
    late = (e // 4) % 2 == 1
    early = jnp.logical_not(late)
    partner = e + OFF - 2 * OFF * upper
    up = (e + 2 * OFF) % energies
    down = (e + energies - 2 * OFF) % energies
    y_to = jnp.where(upper == 0, down, up)
    q_to = jnp.where(upper == 0, up, down)
    left = (s + slabs - 1) % slabs
    right = (s + 1) % slabs

    has_up = e + 2 * OFF < energies
    has_down = e >= 2 * OFF
    has_left = s > 0
    has_right = s < slabs - 1
    y_in = jnp.where(upper == 0, has_up, has_down)
    y_out = jnp.where(upper == 0, has_down, has_up)
    q_in, q_out = y_out, y_in

    def when(flag, action):
        @pl.when(flag)
        def _():
            action()

    def signal(semaphore, device):
        pl.semaphore_signal(semaphore, inc=1, device_id=device, device_id_type=MESH)

    barrier = pltpu.get_barrier_semaphore()
    signal(barrier, (partner, s))
    for flag, device in (
        (has_up, (up, s)), (has_down, (down, s)), (has_left, (e, left)), (has_right, (e, right)),
    ):
        when(flag, lambda device=device: signal(barrier, device))
    n_peers = 1 + sum(flag.astype(jnp.int32) for flag in (has_up, has_down, has_left, has_right))

    blocks = (c0, c1, c2, c3)
    small = [
        pltpu.make_async_copy(src, dst, small_sem.at[i])
        for i, (src, dst) in enumerate(((bonds_hbm, bonds), (counts_hbm, counts), (bose_hbm, bose)))
    ]
    for copy in small:
        copy.start()
    load_g = [pltpu.make_async_copy(green.at[0, b], g.at[b], load_sem.at[b]) for b in range(4)]
    load_c = {b: pltpu.make_async_copy(coupling.at[b], blocks[b], load_sem.at[4 + b]) for b in (0, 2, 3)}
    early_c = [pltpu.make_async_copy(coupling.at[1, k], c1.at[k], first_sem.at[k]) for k in range(3)]
    for copy in (load_g[1], early_c[0], load_g[0], early_c[1], early_c[2], load_g[2]):
        copy.start()

    def remote(src, dst, send, recv, device):
        return pltpu.make_async_remote_copy(
            src_ref=src, dst_ref=dst, send_sem=send, recv_sem=recv,
            device_id=device, device_id_type=MESH,
        )

    to_right = remote(green.at[0, 3], before, halo_send.at[0], halo_recv.at[0], (e, right))
    to_left = remote(green.at[0, 0], after, halo_send.at[1], halo_recv.at[1], (e, left))
    edge_before = pltpu.make_async_copy(green.at[0, 1], before, halo_recv.at[0])
    edge_after = pltpu.make_async_copy(green.at[0, 2], after, halo_recv.at[1])
    count = remote(cnt_own, cnt_got, cnt_sem.at[0], cnt_sem.at[1], (partner, s))

    def rows_of(t):
        return t // per, pl.ds(pl.multiple_of((t % per) * ROWS, ROWS), ROWS)

    def block_of(j):
        return jnp.where(j < 2, j + 1, jnp.where(j == 2, 0, 3))

    def z_copy(t):
        j, r = rows_of(t)
        return remote(part.at[j, r], got_z.at[j, r], z_send.at[t], z_recv.at[t], (partner, s))

    def q_copy(t):
        j, r = rows_of(t)
        return remote(got_z.at[j, r], got_q.at[j, r], q_send.at[t], q_recv.at[t], (q_to, s))

    def y_copy(t):
        j, r = rows_of(t)
        return remote(part.at[j, r], got_y.at[j, r], y_send.at[t], y_recv.at[t], (y_to, s))

    def o_copy(t):
        j, r = rows_of(t)
        return remote(sig.at[j, r], sigma.at[0, block_of(j), r], o_send.at[t], o_recv.at[t], (partner, s))

    def z_first(t):
        return jnp.where(early, t // per != 2, t // per == 0)

    def loop(first, last, body):
        def step(t, _):
            body(t)
            return 0

        lax.fori_loop(first, last, step, 0)

    def term(c, k, r, near):
        half = jnp.dot(c[k, r, :], near[...], preferred_element_type=jnp.float32)
        return lax.dot_general(
            half.astype(jnp.bfloat16), c[k], (((1,), (1,)), ((), ())),
            preferred_element_type=jnp.float32,
        )

    def products(b, r, lower, higher, ready=None):
        c = blocks[b]
        total = term(c, 0, r, g.at[b])
        if ready is not None:
            ready()
        k = 1 + (bonds[b, 1] > bonds[b, 0]).astype(jnp.int32)
        total = total + term(c, k, r, lower)
        total = total + term(c, 3 - k, r, higher)
        return total.astype(jnp.bfloat16)

    def rest():
        for copy in small + early_c[1:] + [load_g[0], load_g[2]]:
            copy.wait()
        for copy in (load_c[2], load_g[3], load_c[0], load_c[3]):
            copy.start()

    def first_sends():
        cnt_own[...] = jnp.full(cnt_own.shape, counts[0], jnp.int32)
        when(has_right, to_right.start)
        when(has_left, to_left.start)
        count.start()

    def work(j, lower, higher, send=None, start=0):
        rows = CHUNK[j]

        def chunk(i):
            r = pl.ds(pl.multiple_of(i * rows, rows), rows)
            part[j, r, :] = products(ORDER[j], r, lower, higher)
            if send is not None:
                first = j * per + i * (rows // ROWS)
                loop(first, first + rows // ROWS, send)

        loop(start, orb // rows, chunk)

    def forward(t):
        z_copy(t).wait_recv()
        when(q_out, q_copy(t).start)

    load_g[1].wait()
    early_c[0].wait()
    top = pl.ds(0, CHUNK[0])
    part[0, top, :] = products(1, top, g.at[0], g.at[2], rest)
    pl.semaphore_wait(barrier, n_peers)
    loop(0, CHUNK[0] // ROWS, lambda t: z_copy(t).start())
    first_sends()
    work(0, g.at[0], g.at[2], lambda t: z_copy(t).start(), 1)
    load_g[3].wait()
    load_c[2].wait()
    work(1, g.at[1], g.at[3], lambda t: when(early, z_copy(t).start))
    when(s == 0, edge_before.start)
    when(s == slabs - 1, edge_after.start)
    to_right.wait_recv()
    to_left.wait_recv()
    when(y_in, lambda: signal(y_ok, (q_to, s)))
    when(q_in, lambda: signal(q_ok, (y_to, s)))
    load_c[0].wait()
    work(2, before, g.at[1])
    when(y_out, lambda: pl.semaphore_wait(y_ok, 1))
    when(q_out, lambda: pl.semaphore_wait(q_ok, 1))
    when(jnp.logical_and(late, y_out), lambda: loop(per, 2 * per, lambda t: y_copy(t).start()))
    when(y_out, lambda: loop(2 * per, 3 * per, lambda t: y_copy(t).start()))
    when(early, lambda: loop(0, 3, forward))
    load_c[3].wait()
    work(3, g.at[2], after, lambda t: (
        when(early, z_copy(t).start), when(jnp.logical_and(late, y_out), y_copy(t).start)
    ))

    n = bose[0]
    y_own, y_far = jnp.where(upper == 0, n, n + 1.0), jnp.where(upper == 0, n + 1.0, n)
    q_own, q_far = y_far, y_own

    def combine(target, terms, cnt, block):
        total = sum(factor * value.astype(jnp.float32) for factor, value in terms)
        target[...] = jnp.where(cnt[0:1, :] > block, total, 0.0).astype(jnp.bfloat16)

    def across(t):
        j, r = rows_of(t)
        own = (y_own, part[j, r, :])
        block = s * 4 + block_of(j)

        def both():
            y_copy(t).wait_recv()
            combine(sig.at[j, r], (own, (y_far, got_y[j, r, :])), cnt_got, block)

        when(y_in, both)
        when(jnp.logical_not(y_in), lambda: combine(sig.at[j, r], (own,), cnt_got, block))
        o_copy(t).start()

    count.wait_recv()
    period = 2 * per

    def early_part():
        loop(3, 8, forward)
        loop(8, 10, across)
        loop(12, 14, forward)
        loop(10, 12, across)
        loop(14, 16, forward)

    def late_part():
        loop(0, 2, forward)
        loop(2, 4, lambda t: (across(t + 2), forward(t)))
        loop(6, 16, across)

    when(early, early_part)
    when(late, late_part)

    def keep(t):
        j, r = rows_of(t)
        target = sigma.at[0, block_of(j), r]
        block = s * 4 + block_of(j)

        def both():
            q_copy(t).wait_recv()
            combine(target, ((q_own, got_z[j, r, :]), (q_far, got_q[j, r, :])), cnt_own, block)

        when(q_in, both)
        when(jnp.logical_not(q_in), lambda: combine(target, ((q_own, got_z[j, r, :]),), cnt_own, block))

    loop(0, 2 * period, lambda t: when(z_first(t), lambda: keep(t)))

    when(has_right, to_right.wait_send)
    when(has_left, to_left.wait_send)
    count.wait_send()

    def finish(t):
        def z_way():
            z_copy(t).wait_send()
            when(q_out, q_copy(t).wait_send)

        def y_way():
            when(y_out, y_copy(t).wait_send)
            o_copy(t).wait_send()
            o_copy(t).wait_recv()

        when(z_first(t), z_way)
        when(jnp.logical_not(z_first(t)), y_way)

    loop(0, 2 * period, finish)


def solution(mesh):
    energies, slabs = mesh.shape["energy"], mesh.shape["slab"]

    def on_device(green, coupling, bonds, counts, bose):
        orb = green.shape[-1]
        tiles = 4 * (orb // ROWS)
        block = (orb, orb)
        dma = pltpu.SemaphoreType.DMA
        whole = pltpu.VMEM((4,) + block, jnp.bfloat16)
        hbm = pl.BlockSpec(memory_space=pltpu.HBM)
        return pl.pallas_call(
            functools.partial(kernel, energies, slabs),
            out_shape=pltpu.VMEM(green.shape, jnp.bfloat16),
            in_specs=[hbm] * 5,
            out_specs=pl.BlockSpec(memory_space=pltpu.VMEM),
            scratch_shapes=[
                whole,
                pltpu.VMEM(block, jnp.bfloat16),
                pltpu.VMEM(block, jnp.bfloat16),
            ]
            + [pltpu.VMEM((3,) + block, jnp.bfloat16)] * 4
            + [whole] * 5
            + [pltpu.VMEM((8, orb), jnp.int32)] * 2
            + [pltpu.SMEM(bonds.shape, jnp.int32), pltpu.SMEM((1,), jnp.int32), pltpu.SMEM((1,), jnp.float32)]
            + [dma((8,)), dma((3,)), dma((3,)), dma((2,)), dma((2,)), dma((2,))] + [pltpu.SemaphoreType.REGULAR] * 2
            + [dma((tiles,))] * 8,
            compiler_params=pltpu.CompilerParams(
                collective_id=0, has_side_effects=True, vmem_limit_bytes=60 * MIB
            ),
            cost_estimate=pl.CostEstimate(
                flops=48 * orb**3, bytes_accessed=20 * MIB, transcendentals=0
            ),
            name="self_energy",
        )(green, coupling, bonds, counts, bose)

    return jax.shard_map(
        on_device,
        mesh=mesh,
        in_specs=(
            P("energy", "slab", None, None),
            P("slab", None, None, None),
            P("slab", None),
            P("energy"),
            P(),
        ),
        out_specs=P("energy", "slab", None, None),
        check_vma=False,
    )
```

```python
import functools

import jax
import jax.numpy as jnp
from jax import lax
from jax.experimental import pallas as pl
from jax.experimental.pallas import tpu as pltpu
from jax.sharding import PartitionSpec as P

OFF = 8
ROWS = 128
MESH = pl.DeviceIdType.MESH
MIB = 2**20
ORDER = (1, 2, 0, 3)
CHUNK = (128, 512, 512, 512)


def kernel(
    energies, slabs,
    green, coupling, bonds_hbm, counts_hbm, bose_hbm, sigma,
    g, before, after, c0, c1, c2, c3,
    part, got_z, got_q, got_y, sig, cnt_own, cnt_got, bonds, counts, bose,
    load_sem, first_sem, small_sem, halo_send, halo_recv, cnt_sem, y_ok, q_ok,
    z_send, z_recv, q_send, q_recv, y_send, y_recv, o_send, o_recv,
):
    e = lax.axis_index("energy")
    s = lax.axis_index("slab")
    orb = g.shape[-1]
    per = orb // ROWS
    upper = (e // OFF) % 2
    late = (e // 4) % 2 == 1
    early = jnp.logical_not(late)
    partner = e + OFF - 2 * OFF * upper
    up = (e + 2 * OFF) % energies
    down = (e + energies - 2 * OFF) % energies
    y_to = jnp.where(upper == 0, down, up)
    q_to = jnp.where(upper == 0, up, down)
    left = (s + slabs - 1) % slabs
    right = (s + 1) % slabs

    has_up = e + 2 * OFF < energies
    has_down = e >= 2 * OFF
    has_left = s > 0
    has_right = s < slabs - 1
    y_in = jnp.where(upper == 0, has_up, has_down)
    y_out = jnp.where(upper == 0, has_down, has_up)
    q_in, q_out = y_out, y_in

    def when(flag, action):
        @pl.when(flag)
        def _():
            action()

    def signal(semaphore, device):
        pl.semaphore_signal(semaphore, inc=1, device_id=device, device_id_type=MESH)

    barrier = pltpu.get_barrier_semaphore()
    signal(barrier, (partner, s))
    for flag, device in (
        (has_up, (up, s)), (has_down, (down, s)), (has_left, (e, left)), (has_right, (e, right)),
    ):
        when(flag, lambda device=device: signal(barrier, device))
    n_peers = 1 + sum(flag.astype(jnp.int32) for flag in (has_up, has_down, has_left, has_right))

    blocks = (c0, c1, c2, c3)
    small = [
        pltpu.make_async_copy(src, dst, small_sem.at[i])
        for i, (src, dst) in enumerate(((bonds_hbm, bonds), (counts_hbm, counts), (bose_hbm, bose)))
    ]
    for copy in small:
        copy.start()
    load_g = [pltpu.make_async_copy(green.at[0, b], g.at[b], load_sem.at[b]) for b in range(4)]
    load_c = {b: pltpu.make_async_copy(coupling.at[b], blocks[b], load_sem.at[4 + b]) for b in (0, 2, 3)}
    early_c = [pltpu.make_async_copy(coupling.at[1, k], c1.at[k], first_sem.at[k]) for k in range(3)]
    for copy in (load_g[1], early_c[0], load_g[0], early_c[1], early_c[2], load_g[2]):
        copy.start()

    def remote(src, dst, send, recv, device):
        return pltpu.make_async_remote_copy(
            src_ref=src, dst_ref=dst, send_sem=send, recv_sem=recv,
            device_id=device, device_id_type=MESH,
        )

    to_right = remote(green.at[0, 3], before, halo_send.at[0], halo_recv.at[0], (e, right))
    to_left = remote(green.at[0, 0], after, halo_send.at[1], halo_recv.at[1], (e, left))
    edge_before = pltpu.make_async_copy(green.at[0, 1], before, halo_recv.at[0])
    edge_after = pltpu.make_async_copy(green.at[0, 2], after, halo_recv.at[1])
    count = remote(cnt_own, cnt_got, cnt_sem.at[0], cnt_sem.at[1], (partner, s))

    def rows_of(t):
        return t // per, pl.ds(pl.multiple_of((t % per) * ROWS, ROWS), ROWS)

    def block_of(j):
        return jnp.where(j < 2, j + 1, jnp.where(j == 2, 0, 3))

    def z_copy(t):
        j, r = rows_of(t)
        return remote(part.at[j, r], got_z.at[j, r], z_send.at[t], z_recv.at[t], (partner, s))

    def q_copy(t):
        j, r = rows_of(t)
        return remote(got_z.at[j, r], got_q.at[j, r], q_send.at[t], q_recv.at[t], (q_to, s))

    def y_copy(t):
        j, r = rows_of(t)
        return remote(part.at[j, r], got_y.at[j, r], y_send.at[t], y_recv.at[t], (y_to, s))

    def o_copy(t):
        j, r = rows_of(t)
        return remote(sig.at[j, r], sigma.at[0, block_of(j), r], o_send.at[t], o_recv.at[t], (partner, s))

    def z_first(t):
        return jnp.where(early, t // per != 2, t // per == 0)

    def loop(first, last, body):
        def step(t, _):
            body(t)
            return 0

        lax.fori_loop(first, last, step, 0)

    def term(c, k, r, near):
        half = jnp.dot(c[k, r, :], near[...], preferred_element_type=jnp.float32)
        return lax.dot_general(
            half.astype(jnp.bfloat16), c[k], (((1,), (1,)), ((), ())),
            preferred_element_type=jnp.float32,
        )

    def products(b, r, lower, higher, ready=None):
        c = blocks[b]
        total = term(c, 0, r, g.at[b])
        if ready is not None:
            ready()
        k = 1 + (bonds[b, 1] > bonds[b, 0]).astype(jnp.int32)
        total = total + term(c, k, r, lower)
        total = total + term(c, 3 - k, r, higher)
        return total.astype(jnp.bfloat16)

    def rest():
        for copy in small + early_c[1:] + [load_g[0], load_g[2]]:
            copy.wait()
        for copy in (load_c[2], load_g[3], load_c[0], load_c[3]):
            copy.start()

    def first_sends():
        cnt_own[...] = jnp.full(cnt_own.shape, counts[0], jnp.int32)
        when(has_right, to_right.start)
        when(has_left, to_left.start)
        count.start()

    def work(j, lower, higher, send=None, start=0):
        rows = CHUNK[j]

        def chunk(i):
            r = pl.ds(pl.multiple_of(i * rows, rows), rows)
            part[j, r, :] = products(ORDER[j], r, lower, higher)
            if send is not None:
                first = j * per + i * (rows // ROWS)
                loop(first, first + rows // ROWS, send)

        loop(start, orb // rows, chunk)

    def forward(t):
        z_copy(t).wait_recv()
        when(q_out, q_copy(t).start)

    load_g[1].wait()
    early_c[0].wait()
    top = pl.ds(0, CHUNK[0])
    part[0, top, :] = products(1, top, g.at[0], g.at[2], rest)
    pl.semaphore_wait(barrier, n_peers)
    loop(0, CHUNK[0] // ROWS, lambda t: z_copy(t).start())
    first_sends()
    work(0, g.at[0], g.at[2], lambda t: z_copy(t).start(), 1)
    load_g[3].wait()
    load_c[2].wait()
    work(1, g.at[1], g.at[3], lambda t: when(early, z_copy(t).start))
    when(s == 0, edge_before.start)
    when(s == slabs - 1, edge_after.start)
    to_right.wait_recv()
    to_left.wait_recv()
    when(y_in, lambda: signal(y_ok, (q_to, s)))
    when(q_in, lambda: signal(q_ok, (y_to, s)))
    load_c[0].wait()
    work(2, before, g.at[1])
    when(y_out, lambda: pl.semaphore_wait(y_ok, 1))
    when(q_out, lambda: pl.semaphore_wait(q_ok, 1))
    when(jnp.logical_and(late, y_out), lambda: loop(per, 2 * per, lambda t: y_copy(t).start()))
    when(y_out, lambda: loop(2 * per, 3 * per, lambda t: y_copy(t).start()))
    load_c[3].wait()
    work(3, g.at[2], after, lambda t: (
        when(early, z_copy(t).start), when(jnp.logical_and(late, y_out), y_copy(t).start)
    ))

    n = bose[0]
    y_own, y_far = jnp.where(upper == 0, n, n + 1.0), jnp.where(upper == 0, n + 1.0, n)
    q_own, q_far = y_far, y_own

    def combine(target, terms, cnt, block):
        total = sum(factor * value.astype(jnp.float32) for factor, value in terms)
        target[...] = jnp.where(cnt[0:1, :] > block, total, 0.0).astype(jnp.bfloat16)

    def across(t):
        j, r = rows_of(t)
        own = (y_own, part[j, r, :])
        block = s * 4 + block_of(j)

        def both():
            y_copy(t).wait_recv()
            combine(sig.at[j, r], (own, (y_far, got_y[j, r, :])), cnt_got, block)

        when(y_in, both)
        when(jnp.logical_not(y_in), lambda: combine(sig.at[j, r], (own,), cnt_got, block))
        o_copy(t).start()

    count.wait_recv()
    period = 2 * per

    def early_part():
        loop(0, 6, forward)
        loop(8, 10, across)
        loop(6, 8, forward)
        loop(10, 12, across)
        loop(12, 16, forward)

    def late_part():
        loop(4, 8, across)
        loop(0, 4, forward)
        loop(8, 16, across)

    when(early, early_part)
    when(late, late_part)

    def keep(t):
        j, r = rows_of(t)
        target = sigma.at[0, block_of(j), r]
        block = s * 4 + block_of(j)

        def both():
            q_copy(t).wait_recv()
            combine(target, ((q_own, got_z[j, r, :]), (q_far, got_q[j, r, :])), cnt_own, block)

        when(q_in, both)
        when(jnp.logical_not(q_in), lambda: combine(target, ((q_own, got_z[j, r, :]),), cnt_own, block))

    loop(0, 2 * period, lambda t: when(z_first(t), lambda: keep(t)))

    when(has_right, to_right.wait_send)
    when(has_left, to_left.wait_send)
    count.wait_send()

    def finish(t):
        def z_way():
            z_copy(t).wait_send()
            when(q_out, q_copy(t).wait_send)

        def y_way():
            when(y_out, y_copy(t).wait_send)
            o_copy(t).wait_send()
            o_copy(t).wait_recv()

        when(z_first(t), z_way)
        when(jnp.logical_not(z_first(t)), y_way)

    loop(0, 2 * period, finish)


def solution(mesh):
    energies, slabs = mesh.shape["energy"], mesh.shape["slab"]

    def on_device(green, coupling, bonds, counts, bose):
        orb = green.shape[-1]
        tiles = 4 * (orb // ROWS)
        block = (orb, orb)
        dma = pltpu.SemaphoreType.DMA
        whole = pltpu.VMEM((4,) + block, jnp.bfloat16)
        hbm = pl.BlockSpec(memory_space=pltpu.HBM)
        return pl.pallas_call(
            functools.partial(kernel, energies, slabs),
            out_shape=pltpu.VMEM(green.shape, jnp.bfloat16),
            in_specs=[hbm] * 5,
            out_specs=pl.BlockSpec(memory_space=pltpu.VMEM),
            scratch_shapes=[
                whole,
                pltpu.VMEM(block, jnp.bfloat16),
                pltpu.VMEM(block, jnp.bfloat16),
            ]
            + [pltpu.VMEM((3,) + block, jnp.bfloat16)] * 4
            + [whole] * 5
            + [pltpu.VMEM((8, orb), jnp.int32)] * 2
            + [pltpu.SMEM(bonds.shape, jnp.int32), pltpu.SMEM((1,), jnp.int32), pltpu.SMEM((1,), jnp.float32)]
            + [dma((8,)), dma((3,)), dma((3,)), dma((2,)), dma((2,)), dma((2,))] + [pltpu.SemaphoreType.REGULAR] * 2
            + [dma((tiles,))] * 8,
            compiler_params=pltpu.CompilerParams(
                collective_id=0, has_side_effects=True, vmem_limit_bytes=60 * MIB
            ),
            cost_estimate=pl.CostEstimate(
                flops=48 * orb**3, bytes_accessed=20 * MIB, transcendentals=0
            ),
            name="self_energy",
        )(green, coupling, bonds, counts, bose)

    return jax.shard_map(
        on_device,
        mesh=mesh,
        in_specs=(
            P("energy", "slab", None, None),
            P("slab", None, None, None),
            P("slab", None),
            P("energy"),
            P(),
        ),
        out_specs=P("energy", "slab", None, None),
        check_vma=False,
    )
```
